256 devices in a mesh: pair: 4 (over x), vir: 64 (over y, z, core).
Axes of the slice: x: 4, y: 4, z: 8, core: 2. Of those that a mesh axis runs over, the one named last changes fastest.
Arguments:
- amplitudes: bfloat16 [768, 768, 768], P(('pair', 'vir')), may hold values from -6 to 6
- integral_tiles: bfloat16 [12288, 128, 128], P(('pair', 'vir')), may hold values from -0.21875 to 0.21875
- need_owner: int32 [27648, 1], P(('pair', 'vir')), may hold values from 0 to 255, as said below
- need_slot: int32 [27648, 1], P(('pair', 'vir')), may hold values from 0 to 47
- pair_occ: int32 [768, 2], P(('pair', 'vir')), may hold values from 0 to 399
- domain: int32 [768, 6], P(('pair', 'vir')), may hold values from 0 to 24, as said below
- eps_occ: float32 [400], replicated, may hold values from -2 to -0.3
- eps_vir: float32 [3200], replicated, may hold values from 0.2 to 6
Outputs:
- residual: float32 [768, 768, 768], P(('pair', 'vir'))
The draws below stay inside these ranges and needn't reach their ends.
Inputs may be any that keep to these rules, and one draw needn't show every extreme that they name: `need_owner`: write a holder as h = q * 64 + v with v its vir index; among the requests of one device's pairs no v is named more than 3 times, and on every device some v is named exactly 3 times. `domain`: each row names 6 different tiles.
All inputs are finite; a program needn't handle non-finite values.
Results may differ from the reference program's by a relative error of at most 0.0031.
Values may be sent and summed in bfloat16 or wider, within the bound.
No kernel may reach another device: no remote copies, remote signals or barrier semaphores. Data moves between devices by JAX's collectives and lax.ppermute only.
A program may use at most 192 MiB of HBM per device.

```python
import math
import jax
import jax.numpy as jnp
from jax import lax

TILE = 128
NVIR = 3200
NOCC = 400
NVT = 25
ND = 6
XT_DEV = 48
PAIRS = 768
REQ_DEV = 108
REQS = 27648
XTILES = 12288
COLCAP = 3
N_PAIR = 4
N_VIR = 64
DEVICES = 256


def draw_domain(key, part):
    keys = jax.random.split(key, PAIRS)
    chosen = jax.vmap(lambda single: jax.random.permutation(single, NVT)[:ND])(keys)
    return chosen.astype(jnp.int32)


def draw_need_owner(key, part):
    keys = jax.random.split(key, DEVICES)
    total = N_VIR * COLCAP

    def one_device(single):
        key_one, key_two, key_three, key_four = jax.random.split(single, 4)
        scores = jax.random.permutation(key_one, total).astype(jnp.int32)
        first = jax.random.randint(key_two, (), 0, N_VIR)
        slot_ids = jnp.arange(total, dtype=jnp.int32)
        scores = jnp.where(slot_ids // COLCAP == first, slot_ids % COLCAP - COLCAP, scores)
        order = jnp.argsort(scores, stable=True)[:REQ_DEV].astype(jnp.int32)
        order = order[jax.random.permutation(key_three, REQ_DEV)]
        column = (order // COLCAP).astype(jnp.int32)
        row_pick = jax.random.randint(key_four, (REQ_DEV,), 0, N_PAIR).astype(jnp.int32)
        return row_pick * N_VIR + column
    return jax.vmap(one_device)(keys).reshape(REQS, 1).astype(jnp.int32)


def set_ends(values, key, low, top_value):
    spot = [jax.random.randint(jax.random.fold_in(key, axis), (), 0, length) for axis, length in enumerate(values.shape)]
    widest = values.shape.index(max(values.shape))
    neighbour = spot[:widest] + [(spot[widest] + 1) % values.shape[widest]] + spot[widest + 1:]
    return values.at[tuple(spot)].set(low).at[tuple(neighbour)].set(top_value)


def levels(key, dims, shards, smallest, high):
    factor_of = 1.0
    for axis_at, parts in shards:
        steps = jax.random.uniform(jax.random.fold_in(jax.random.fold_in(key, 6), axis_at), (parts,), jnp.float32, smallest / len(shards), high / len(shards))
        factor_of = factor_of * jnp.repeat(jnp.exp(steps), dims[axis_at] // parts).reshape((-1,) + (1,) * (len(dims) - 1 - axis_at))
    return factor_of


def gaussian(key, dims, deviation, most, cuts=(), kind=jnp.bfloat16):
    drawn = deviation * jax.random.normal(key, dims, jnp.float32)
    if cuts:
        drawn = drawn * levels(key, dims, cuts, -0.22, 0.18)
    return jnp.clip(drawn, -most, most).astype(kind)


def setup_inputs(seed: int = 0) -> dict:
    arg_keys = jax.random.split(jax.random.key(seed), 9)
    return {
        "amplitudes": gaussian(arg_keys[0], (PAIRS, ND * TILE, ND * TILE), 1.0, 6.0, ((0, 256),)),
        "integral_tiles": gaussian(arg_keys[1], (XTILES, TILE, TILE), (ND * TILE) ** -0.5, 0.21875, ((0, 256),)),
        "need_owner": draw_need_owner(jax.random.fold_in(arg_keys[8], 71), 0),
        "need_slot": set_ends(jax.random.randint(arg_keys[3], (REQS, 1), 0, XT_DEV), jax.random.fold_in(arg_keys[3], 1), 0, XT_DEV - 1).astype(jnp.int32),
        "pair_occ": set_ends(jax.random.randint(arg_keys[4], (PAIRS, 2), 0, NOCC), jax.random.fold_in(arg_keys[4], 1), 0, NOCC - 1).astype(jnp.int32),
        "domain": draw_domain(jax.random.fold_in(arg_keys[8], 71), 0),
        "eps_occ": jnp.clip(jax.random.uniform(arg_keys[6], (NOCC,), jnp.float32, -2.0, -0.3), -2.0, -0.3),
        "eps_vir": jnp.clip(jnp.exp(jax.random.uniform(arg_keys[7], (NVIR,), jnp.float32, math.log(0.2), math.log(6.0))), 0.2, 6.0),
    }


def reference(amplitudes, integral_tiles, need_owner, need_slot, pair_occ, domain, eps_occ, eps_vir):
    index_table = (need_owner[:, 0] * XT_DEV + need_slot[:, 0]).astype(jnp.int32).reshape(PAIRS, ND * ND)
    vir_table = eps_vir.reshape(NVT, TILE)

    def one_pair(packed):
        amp_block, tile_index, occ_pair, dom_row = packed
        gathered = integral_tiles[tile_index].reshape(ND, ND, TILE, TILE)
        blocks = gathered.transpose(0, 2, 1, 3).reshape(ND * TILE, ND * TILE)
        mixed = (2.0 * amp_block.astype(jnp.float32) - amp_block.T.astype(jnp.float32)).astype(jnp.bfloat16)
        cycle_term = jnp.dot(mixed, blocks, preferred_element_type=jnp.float32) + jnp.dot(blocks.T, mixed, preferred_element_type=jnp.float32)
        vir_energy = vir_table[dom_row].reshape(ND * TILE)
        occ_total = eps_occ[occ_pair[0]] + eps_occ[occ_pair[1]]
        denominator = occ_total - vir_energy[:, None] - vir_energy[None, :]
        return cycle_term / denominator

    return lax.map(one_pair, (amplitudes, index_table, pair_occ, domain))
```

```python
import functools

import jax
import jax.numpy as jnp
from jax import lax
from jax.experimental import pallas as pl
from jax.experimental.pallas import tpu as pltpu
from jax.sharding import PartitionSpec as P

ROWS_FIRST = 32
PER_COLUMN = 3
ANY = pl.BlockSpec(memory_space=pl.ANY)
SMEM = pl.BlockSpec(memory_space=pltpu.SMEM)
BIG = 100 * 2**20 // 2


def split_kernel(row_from, tiles_ref, after_ref, low_ref, high_ref, sem):
    half, rows = low_ref.shape[0], low_ref.shape[1]
    first = pltpu.make_async_copy(
        tiles_ref.at[pl.ds(0, half), pl.ds(row_from, rows)], low_ref, sem.at[0]
    )
    second = pltpu.make_async_copy(
        tiles_ref.at[pl.ds(half, half), pl.ds(row_from, rows)], high_ref, sem.at[1]
    )
    first.start()
    second.start()
    first.wait()
    second.wait()


def split(tiles, after, row_from, rows):
    half = tiles.shape[0] // 2
    shape = jax.ShapeDtypeStruct((half, rows, tiles.shape[2]), tiles.dtype)
    return pl.pallas_call(
        functools.partial(split_kernel, row_from),
        out_shape=(shape, shape),
        in_specs=[ANY, ANY],
        out_specs=(ANY, ANY),
        scratch_shapes=[pltpu.SemaphoreType.DMA((2,))],
        cost_estimate=pl.CostEstimate(
            flops=0, bytes_accessed=4 * half * rows * 128 * 2, transcendentals=0
        ),
        name="split_rows",
    )(tiles, after)


def serve_kernel(row_from, code_ref, tiles_ref, *refs):
    sources, out_ref, sem = refs[:6], refs[6], refs[7]
    half = tiles_ref.shape[0] // 2
    rows = out_ref.shape[1]

    def step(slot, carry):
        code = code_ref[slot]
        place = code & 31

        def own():
            pltpu.make_async_copy(
                tiles_ref.at[place + half * ((code >> 5) & 1), pl.ds(row_from, rows)],
                out_ref.at[slot],
                sem,
            ).start()

        def other(source):
            pltpu.make_async_copy(source.at[place], out_ref.at[slot], sem).start()

        lax.switch(
            code >> 5,
            [own, own] + [functools.partial(other, source) for source in sources],
        )
        return carry

    lax.fori_loop(0, out_ref.shape[0], step, 0)
    pltpu.make_async_copy(out_ref, out_ref, sem).wait()


def serve(codes, tiles, sources, row_from, rows):
    slots = codes.shape[0]
    return pl.pallas_call(
        functools.partial(serve_kernel, row_from),
        out_shape=jax.ShapeDtypeStruct((slots, rows, tiles.shape[2]), tiles.dtype),
        in_specs=[SMEM] + [ANY] * 7,
        out_specs=ANY,
        scratch_shapes=[pltpu.SemaphoreType.DMA],
        cost_estimate=pl.CostEstimate(
            flops=0, bytes_accessed=2 * slots * rows * 128 * 2, transcendentals=0
        ),
        name="serve_tiles",
    )(codes, tiles, *sources)


def gather_pairs(low, high):
    n = lax.axis_size("pair")
    up = [(i, (i + 1) % n) for i in range(n)]
    down = [(i, (i + n - 1) % n) for i in range(n)]
    up_low = lax.ppermute(low, "pair", up)
    down_high = lax.ppermute(high, "pair", down)
    up_high = lax.ppermute(high, "pair", up)
    down_low = lax.ppermute(low, "pair", down)
    far_low = lax.ppermute(up_low, "pair", up)
    far_high = lax.ppermute(down_high, "pair", down)
    return down_low, down_high, far_low, far_high, up_low, up_high


def mix_kernel(amp_ref, after_ref, mixed_ref):
    amp = amp_ref[0]
    mixed_ref[0] = (
        2.0 * amp.astype(jnp.float32) - jnp.transpose(amp).astype(jnp.float32)
    ).astype(mixed_ref.dtype)


def mix(amplitudes, after):
    pairs, width, _ = amplitudes.shape
    spec = pl.BlockSpec((1, width, width), lambda p: (p, 0, 0))
    return pl.pallas_call(
        mix_kernel,
        grid=(pairs,),
        out_shape=jax.ShapeDtypeStruct(amplitudes.shape, amplitudes.dtype),
        in_specs=[spec, ANY],
        out_specs=spec,
        cost_estimate=pl.CostEstimate(
            flops=pairs * width * width, bytes_accessed=4 * pairs * width * width, transcendentals=0
        ),
        compiler_params=pltpu.CompilerParams(vmem_limit_bytes=BIG),
        name="mix_amplitudes",
    )(amplitudes, after)


def residual_kernel(
    rows_first, tile, place_ref, occ_ref, domain_ref, eps_occ_ref, eps_vir_ref,
    mixed_ref, first_ref, second_ref, out_ref, block, sem,
):
    pair = pl.program_id(0)
    pairs = pl.num_programs(0)
    width = out_ref.shape[2]
    count = width // tile

    def fetch(which):
        slot = which % 2

        def step(k, carry):
            row = pl.multiple_of((k // count) * tile, tile)
            column = pl.ds(pl.multiple_of((k % count) * tile, tile), tile)
            place = place_ref[which * count * count + k]
            pltpu.make_async_copy(
                first_ref.at[place], block.at[slot, pl.ds(row, rows_first), column], sem.at[slot]
            ).start()
            pltpu.make_async_copy(
                second_ref.at[place],
                block.at[slot, pl.ds(row + rows_first, tile - rows_first), column],
                sem.at[slot],
            ).start()
            return carry

        lax.fori_loop(0, count * count, step, 0)

    @pl.when(pair == 0)
    def _():
        fetch(0)

    @pl.when(pair + 1 < pairs)
    def _():
        fetch(pair + 1)

    now = pair % 2
    pltpu.make_async_copy(block.at[now], block.at[now], sem.at[now]).wait()

    occ = eps_occ_ref[occ_ref[2 * pair]] + eps_occ_ref[occ_ref[2 * pair + 1]]
    energies = [
        eps_vir_ref[pl.ds(domain_ref[count * pair + c], 1), :] for c in range(count)
    ]
    across = jnp.concatenate(energies, axis=1)
    for c in range(0, count, 2):
        part = pl.ds(c * tile, 2 * tile)
        down = jnp.transpose(
            jnp.broadcast_to(jnp.concatenate(energies[c : c + 2], axis=1), (8, 2 * tile))
        )[:, :1]
        total = jnp.dot(
            mixed_ref[0, part, :], block[now], preferred_element_type=jnp.float32
        )
        total = total + lax.dot_general(
            block[now, :, part],
            mixed_ref[0],
            (((0,), (0,)), ((), ())),
            preferred_element_type=jnp.float32,
        )
        out_ref[0, part, :] = total / (occ - down - across)


def residual(places, pair_occ, domain, eps_occ, eps_vir, mixed, first, second):
    pairs, width, _ = mixed.shape
    rows_first, tile = first.shape[1], first.shape[2]
    return pl.pallas_call(
        functools.partial(residual_kernel, rows_first, tile),
        grid=(pairs,),
        out_shape=jax.ShapeDtypeStruct(mixed.shape, jnp.float32),
        in_specs=[
            SMEM,
            SMEM,
            SMEM,
            SMEM,
            pl.BlockSpec(memory_space=pltpu.VMEM),
            pl.BlockSpec((1, width, width), lambda p: (p, 0, 0)),
            ANY,
            ANY,
        ],
        out_specs=pl.BlockSpec((1, width, width), lambda p: (p, 0, 0)),
        scratch_shapes=[
            pltpu.VMEM((2, width, width), mixed.dtype),
            pltpu.SemaphoreType.DMA((2,)),
        ],
        cost_estimate=pl.CostEstimate(
            flops=4 * pairs * width**3, bytes_accessed=8 * pairs * width**2, transcendentals=0
        ),
        compiler_params=pltpu.CompilerParams(vmem_limit_bytes=BIG),
        name="residual",
    )(places, pair_occ, domain, eps_occ, eps_vir, mixed, first, second)


def body(amplitudes, integral_tiles, need_owner, need_slot, pair_occ, domain, eps_occ, eps_vir):
    held, tile, _ = integral_tiles.shape
    half = held // 2
    vir = lax.axis_size("vir")
    n_pair = lax.axis_size("pair")
    owner, slot = need_owner[:, 0], need_slot[:, 0]
    asks = owner.shape[0]
    column = owner % vir
    across = (owner // vir - lax.axis_index("pair") + n_pair) % n_pair
    code = (across * 2 + slot // half) * 32 + slot % half
    order = jnp.arange(asks, dtype=jnp.int32)
    earlier = (column[:, None] == column[None, :]) & (order[None, :] < order[:, None])
    rank = jnp.sum(earlier.astype(jnp.int32), axis=1)
    places = column * PER_COLUMN + rank
    all_slots = jnp.arange(vir * PER_COLUMN, dtype=jnp.int32)
    hits = places[None, :] == all_slots[:, None]
    requests = jnp.sum(jnp.where(hits, code[None, :], 0), axis=1).reshape(vir, PER_COLUMN)
    codes = lax.all_to_all(requests, "vir", split_axis=0, concat_axis=0, tiled=True)
    codes = codes.reshape(vir * PER_COLUMN)

    first = gather_pairs(
        integral_tiles[:half, :ROWS_FIRST], integral_tiles[half:, :ROWS_FIRST]
    )
    low, high = split(integral_tiles, first[0], ROWS_FIRST, tile - ROWS_FIRST)
    second = gather_pairs(low, high)

    served = serve(codes, integral_tiles, first, 0, ROWS_FIRST)
    mixed = mix(amplitudes, served)
    got_first = lax.all_to_all(served, "vir", split_axis=0, concat_axis=0, tiled=True)
    served = serve(codes, integral_tiles, second, ROWS_FIRST, tile - ROWS_FIRST)
    got_second = lax.all_to_all(served, "vir", split_axis=0, concat_axis=0, tiled=True)
    return residual(
        places,
        pair_occ.reshape(-1),
        domain.reshape(-1),
        eps_occ,
        eps_vir.reshape(-1, tile),
        mixed,
        got_first,
        got_second,
    )


def solution(mesh):
    split_both = ("pair", "vir")
    return jax.shard_map(
        body,
        mesh=mesh,
        in_specs=(
            P(split_both, None, None),
            P(split_both, None, None),
            P(split_both, None),
            P(split_both, None),
            P(split_both, None),
            P(split_both, None),
            P(),
            P(),
        ),
        out_specs=P(split_both, None, None),
        check_vma=False,
    )
```

```python
import functools

import jax
import jax.numpy as jnp
from jax import lax
from jax.experimental import pallas as pl
from jax.experimental.pallas import tpu as pltpu
from jax.sharding import PartitionSpec as P

ROWS_FIRST = 32
PER_COLUMN = 3
DEEP = 8
ANY = pl.BlockSpec(memory_space=pl.ANY)
VMEM = pl.BlockSpec(memory_space=pltpu.VMEM)
SMEM = pl.BlockSpec(memory_space=pltpu.SMEM)
BIG = 100 * 2**20 // 2


def ask_kernel(n_pair, half, here_ref, owner_ref, slot_ref, request_ref, place_ref):
    vir = request_ref.shape[0]
    owner, slot = owner_ref[...], slot_ref[...]
    asks = owner.shape[1]
    column = owner % vir
    across = (owner // vir - here_ref[0] + n_pair) % n_pair
    code = (across * 2 + slot // half) * 32 + slot % half
    along = jnp.broadcast_to(column, (asks, asks))
    down = jnp.transpose(along)
    at_row = lax.broadcasted_iota(jnp.int32, (asks, asks), 0)
    at_column = lax.broadcasted_iota(jnp.int32, (asks, asks), 1)
    earlier = jnp.where((along == down) & (at_row < at_column), 1, 0)
    place = column * PER_COLUMN + jnp.sum(earlier, axis=0, keepdims=True)
    place_ref[...] = place
    target = lax.broadcasted_iota(jnp.int32, (vir, asks), 0) * PER_COLUMN
    lane = lax.broadcasted_iota(jnp.int32, (vir, request_ref.shape[2]), 1)
    request = jnp.zeros((vir, request_ref.shape[2]), jnp.int32)
    for k in range(PER_COLUMN):
        asked = jnp.sum(jnp.where(place == target + k, code, 0), axis=1, keepdims=True)
        request = jnp.where(lane == k, asked, request)
    request_ref[...] = jnp.zeros_like(request_ref)
    request_ref[:, 0, :] = request


def ask(here, owner, slot, n_pair, vir, half):
    return pl.pallas_call(
        functools.partial(ask_kernel, n_pair, half),
        out_shape=(
            jax.ShapeDtypeStruct((vir, DEEP, 128), jnp.int32),
            jax.ShapeDtypeStruct(owner.shape, jnp.int32),
        ),
        in_specs=[SMEM, VMEM, VMEM],
        out_specs=(VMEM, VMEM),
        name="make_requests",
    )(here, owner, slot)


def split_kernel(row_from, tiles_ref, after_ref, low_ref, high_ref, sem):
    half, rows = low_ref.shape[0], low_ref.shape[1]
    first = pltpu.make_async_copy(
        tiles_ref.at[pl.ds(0, half), pl.ds(row_from, rows)], low_ref, sem.at[0]
    )
    second = pltpu.make_async_copy(
        tiles_ref.at[pl.ds(half, half), pl.ds(row_from, rows)], high_ref, sem.at[1]
    )
    first.start()
    second.start()
    first.wait()
    second.wait()


def split(tiles, after, row_from, rows):
    half = tiles.shape[0] // 2
    shape = jax.ShapeDtypeStruct((half, rows, tiles.shape[2]), tiles.dtype)
    return pl.pallas_call(
        functools.partial(split_kernel, row_from),
        out_shape=(shape, shape),
        in_specs=[ANY, ANY],
        out_specs=(VMEM, VMEM),
        scratch_shapes=[pltpu.SemaphoreType.DMA((2,))],
        compiler_params=pltpu.CompilerParams(vmem_limit_bytes=BIG),
        cost_estimate=pl.CostEstimate(
            flops=0, bytes_accessed=4 * half * rows * 128 * 2, transcendentals=0
        ),
        name="split_rows",
    )(tiles, after)


def serve_kernel(row_from, code_ref, tiles_ref, *refs):
    sources, (out_ref, code_smem, code_sem, sem) = refs[:6], refs[6:]
    copy = pltpu.make_async_copy(code_ref.at[:, pl.ds(0, 1)], code_smem, code_sem)
    copy.start()
    copy.wait()
    half = tiles_ref.shape[0] // 2
    rows = out_ref.shape[1]

    def step(slot, carry):
        code = code_smem[slot // PER_COLUMN, 0, slot % PER_COLUMN]
        place = code & 31

        def own():
            pltpu.make_async_copy(
                tiles_ref.at[place + half * ((code >> 5) & 1), pl.ds(row_from, rows)],
                out_ref.at[slot],
                sem,
            ).start()

        def other(source):
            pltpu.make_async_copy(source.at[place], out_ref.at[slot], sem).start()

        lax.switch(
            code >> 5,
            [own, own] + [functools.partial(other, source) for source in sources],
        )
        return carry

    lax.fori_loop(0, out_ref.shape[0], step, 0)
    pltpu.make_async_copy(out_ref, out_ref, sem).wait()


def serve(codes, tiles, sources, row_from, rows):
    slots = codes.shape[0] * PER_COLUMN
    return pl.pallas_call(
        functools.partial(serve_kernel, row_from),
        out_shape=jax.ShapeDtypeStruct((slots, rows, tiles.shape[2]), tiles.dtype),
        in_specs=[ANY] * 8,
        out_specs=VMEM,
        scratch_shapes=[
            pltpu.SMEM((codes.shape[0], 1, codes.shape[2]), jnp.int32),
            pltpu.SemaphoreType.DMA,
            pltpu.SemaphoreType.DMA,
        ],
        compiler_params=pltpu.CompilerParams(vmem_limit_bytes=BIG),
        cost_estimate=pl.CostEstimate(
            flops=0, bytes_accessed=2 * slots * rows * 128 * 2, transcendentals=0
        ),
        name="serve_tiles",
    )(codes, tiles, *sources)


def gather_pairs(low, high):
    n = lax.axis_size("pair")
    up = [(i, (i + 1) % n) for i in range(n)]
    down = [(i, (i + n - 1) % n) for i in range(n)]
    up_low = lax.ppermute(low, "pair", up)
    down_high = lax.ppermute(high, "pair", down)
    up_high = lax.ppermute(high, "pair", up)
    down_low = lax.ppermute(low, "pair", down)
    far_low = lax.ppermute(up_low, "pair", up)
    far_high = lax.ppermute(down_high, "pair", down)
    return down_low, down_high, far_low, far_high, up_low, up_high


def mix_kernel(amp_ref, after_ref, mixed_ref):
    amp = amp_ref[0]
    mixed_ref[0] = (
        2.0 * amp.astype(jnp.float32) - jnp.transpose(amp).astype(jnp.float32)
    ).astype(mixed_ref.dtype)


def mix(amplitudes, after):
    pairs, width, _ = amplitudes.shape
    spec = pl.BlockSpec((1, width, width), lambda p: (p, 0, 0))
    return pl.pallas_call(
        mix_kernel,
        grid=(pairs,),
        out_shape=jax.ShapeDtypeStruct(amplitudes.shape, amplitudes.dtype),
        in_specs=[spec, ANY],
        out_specs=spec,
        cost_estimate=pl.CostEstimate(
            flops=pairs * width * width, bytes_accessed=4 * pairs * width * width, transcendentals=0
        ),
        compiler_params=pltpu.CompilerParams(vmem_limit_bytes=BIG),
        name="mix_amplitudes",
    )(amplitudes, after)


def residual_kernel(
    rows_first, tile, place_ref, occ_ref, domain_ref, eps_occ_ref, eps_vir_ref,
    mixed_ref, first_ref, second_ref, out_ref, block, sem,
):
    pair = pl.program_id(0)
    pairs = pl.num_programs(0)
    width = out_ref.shape[2]
    count = width // tile

    def fetch(which):
        slot = which % 2

        def step(k, carry):
            row = pl.multiple_of((k // count) * tile, tile)
            column = pl.ds(pl.multiple_of((k % count) * tile, tile), tile)
            place = place_ref[which * count * count + k]
            pltpu.make_async_copy(
                first_ref.at[place], block.at[slot, pl.ds(row, rows_first), column], sem.at[slot]
            ).start()
            pltpu.make_async_copy(
                second_ref.at[place],
                block.at[slot, pl.ds(row + rows_first, tile - rows_first), column],
                sem.at[slot],
            ).start()
            return carry

        lax.fori_loop(0, count * count, step, 0)

    @pl.when(pair == 0)
    def _():
        fetch(0)

    @pl.when(pair + 1 < pairs)
    def _():
        fetch(pair + 1)

    now = pair % 2
    pltpu.make_async_copy(block.at[now], block.at[now], sem.at[now]).wait()

    occ = eps_occ_ref[occ_ref[2 * pair]] + eps_occ_ref[occ_ref[2 * pair + 1]]
    energies = [
        eps_vir_ref[pl.ds(domain_ref[count * pair + c], 1), :] for c in range(count)
    ]
    across = jnp.concatenate(energies, axis=1)
    for c in range(0, count, 2):
        part = pl.ds(c * tile, 2 * tile)
        down = jnp.transpose(
            jnp.broadcast_to(jnp.concatenate(energies[c : c + 2], axis=1), (8, 2 * tile))
        )[:, :1]
        total = jnp.dot(
            mixed_ref[0, part, :], block[now], preferred_element_type=jnp.float32
        )
        total = total + lax.dot_general(
            block[now, :, part],
            mixed_ref[0],
            (((0,), (0,)), ((), ())),
            preferred_element_type=jnp.float32,
        )
        out_ref[0, part, :] = total / (occ - down - across)


def residual(places, pair_occ, domain, eps_occ, eps_vir, mixed, first, second):
    pairs, width, _ = mixed.shape
    rows_first, tile = first.shape[1], first.shape[2]
    return pl.pallas_call(
        functools.partial(residual_kernel, rows_first, tile),
        grid=(pairs,),
        out_shape=jax.ShapeDtypeStruct(mixed.shape, jnp.float32),
        in_specs=[
            SMEM,
            SMEM,
            SMEM,
            SMEM,
            pl.BlockSpec(memory_space=pltpu.VMEM),
            pl.BlockSpec((1, width, width), lambda p: (p, 0, 0)),
            ANY,
            ANY,
        ],
        out_specs=pl.BlockSpec((1, width, width), lambda p: (p, 0, 0)),
        scratch_shapes=[
            pltpu.VMEM((2, width, width), mixed.dtype),
            pltpu.SemaphoreType.DMA((2,)),
        ],
        cost_estimate=pl.CostEstimate(
            flops=4 * pairs * width**3, bytes_accessed=8 * pairs * width**2, transcendentals=0
        ),
        compiler_params=pltpu.CompilerParams(vmem_limit_bytes=BIG),
        name="residual",
    )(places, pair_occ, domain, eps_occ, eps_vir, mixed, first, second)


def body(amplitudes, integral_tiles, need_owner, need_slot, pair_occ, domain, eps_occ, eps_vir):
    held, tile, _ = integral_tiles.shape
    half = held // 2
    vir = lax.axis_size("vir")
    here = lax.axis_index("pair").astype(jnp.int32).reshape(1)
    requests, places = ask(
        here, need_owner.reshape(1, -1), need_slot.reshape(1, -1), lax.axis_size("pair"), vir, half
    )
    codes = lax.all_to_all(requests, "vir", split_axis=0, concat_axis=0, tiled=True)

    first = gather_pairs(*split(integral_tiles, requests, 0, ROWS_FIRST))
    low, high = split(integral_tiles, first[0], ROWS_FIRST, tile - ROWS_FIRST)
    second = gather_pairs(low, high)

    served = serve(codes, integral_tiles, first, 0, ROWS_FIRST)
    mixed = mix(amplitudes, served)
    got_first = lax.all_to_all(served, "vir", split_axis=0, concat_axis=0, tiled=True)
    served = serve(codes, integral_tiles, second, ROWS_FIRST, tile - ROWS_FIRST)
    got_second = lax.all_to_all(served, "vir", split_axis=0, concat_axis=0, tiled=True)
    return residual(
        places.reshape(-1),
        pair_occ.reshape(-1),
        domain.reshape(-1),
        eps_occ,
        eps_vir.reshape(-1, tile),
        mixed,
        got_first,
        got_second,
    )


def solution(mesh):
    split_both = ("pair", "vir")
    return jax.shard_map(
        body,
        mesh=mesh,
        in_specs=(
            P(split_both, None, None),
            P(split_both, None, None),
            P(split_both, None),
            P(split_both, None),
            P(split_both, None),
            P(split_both, None),
            P(),
            P(),
        ),
        out_specs=P(split_both, None, None),
        check_vma=False,
    )
```

```python
import functools

import jax
import jax.numpy as jnp
from jax import lax
from jax.experimental import pallas as pl
from jax.experimental.pallas import tpu as pltpu
from jax.sharding import PartitionSpec as P

ROWS_FIRST = 32
PER_COLUMN = 3
ANY = pl.BlockSpec(memory_space=pl.ANY)
VMEM = pl.BlockSpec(memory_space=pltpu.VMEM)
SMEM = pl.BlockSpec(memory_space=pltpu.SMEM)
BIG = 100 * 2**20 // 2


def ask_kernel(held, owner_ref, slot_ref, request_ref, place_ref):
    vir = request_ref.shape[0]
    owner, slot = owner_ref[...], slot_ref[...]
    asks = owner.shape[1]
    column = owner % vir
    code = (owner // vir) * held + slot
    along = jnp.broadcast_to(column, (asks, asks))
    down = jnp.transpose(along)
    at_row = lax.broadcasted_iota(jnp.int32, (asks, asks), 0)
    at_column = lax.broadcasted_iota(jnp.int32, (asks, asks), 1)
    earlier = jnp.where((along == down) & (at_row < at_column), 1, 0)
    place = column * PER_COLUMN + jnp.sum(earlier, axis=0, keepdims=True)
    place_ref[...] = place
    target = lax.broadcasted_iota(jnp.int32, (vir, asks), 0) * PER_COLUMN
    request_ref[...] = jnp.concatenate(
        [
            jnp.sum(jnp.where(place == target + k, code, 0), axis=1, keepdims=True)
            for k in range(PER_COLUMN)
        ],
        axis=1,
    )


def ask(owner, slot, vir, held):
    return pl.pallas_call(
        functools.partial(ask_kernel, held),
        out_shape=(
            jax.ShapeDtypeStruct((vir, PER_COLUMN), jnp.int32),
            jax.ShapeDtypeStruct(owner.shape, jnp.int32),
        ),
        in_specs=[VMEM, VMEM],
        out_specs=(VMEM, VMEM),
        name="make_requests",
    )(owner, slot)


def serve_kernel(n_pair, row_from, here_ref, code_ref, own_ref, *refs):
    sources, (out_ref, pool, sem) = refs[: n_pair - 1], refs[n_pair - 1 :]
    held, rows = own_ref.shape[0], out_ref.shape[1]
    copies = []
    for step in range(n_pair):
        owner = (here_ref[0] + step) % n_pair
        source = sources[step - 1] if step else own_ref.at[:, pl.ds(row_from, rows)]
        target = pool.at[pl.ds(owner * held, held)]
        copies.append(pltpu.make_async_copy(source, target, sem.at[step]))
    for copy in copies:
        copy.start()
    for copy in copies:
        copy.wait()
    take(code_ref, pool, out_ref)


def take(code_ref, pool, out_ref):
    def step(column, carry):
        for k in range(PER_COLUMN):
            out_ref[column * PER_COLUMN + k] = pool[code_ref[column, 0, k]]
        return carry

    lax.fori_loop(0, code_ref.shape[0], step, 0, unroll=4)


def serve(here, codes, tiles, sources, row_from, rows):
    slots = codes.shape[0] * PER_COLUMN
    n_pair = len(sources) + 1
    held, tile = tiles.shape[0], tiles.shape[2]
    return pl.pallas_call(
        functools.partial(serve_kernel, n_pair, row_from),
        out_shape=jax.ShapeDtypeStruct((slots, rows, tile), tiles.dtype),
        in_specs=[SMEM, SMEM] + [ANY] * n_pair,
        out_specs=VMEM,
        scratch_shapes=[
            pltpu.VMEM((n_pair * held, rows, tile), tiles.dtype),
            pltpu.SemaphoreType.DMA((n_pair,)),
        ],
        compiler_params=pltpu.CompilerParams(vmem_limit_bytes=BIG),
        cost_estimate=pl.CostEstimate(
            flops=0, bytes_accessed=4 * slots * rows * tile, transcendentals=0
        ),
        name="serve_near",
    )(here, codes, tiles, *sources)


def serve_gathered(codes, gathered):
    slots = codes.shape[0] * PER_COLUMN
    _, rows, tile = gathered.shape
    return pl.pallas_call(
        take,
        out_shape=jax.ShapeDtypeStruct((slots, rows, tile), gathered.dtype),
        in_specs=[SMEM, VMEM],
        out_specs=VMEM,
        compiler_params=pltpu.CompilerParams(vmem_limit_bytes=BIG),
        cost_estimate=pl.CostEstimate(
            flops=0, bytes_accessed=4 * slots * rows * tile, transcendentals=0
        ),
        name="serve_gathered",
    )(codes, gathered)


def from_others(mine):
    n = lax.axis_size("pair")
    return [
        lax.ppermute(mine, "pair", [((i + step) % n, i) for i in range(n)])
        for step in range(1, n)
    ]


def mix_kernel(amp_ref, after_ref, mixed_ref):
    amp = amp_ref[0]
    mixed_ref[0] = (
        2.0 * amp.astype(jnp.float32) - jnp.transpose(amp).astype(jnp.float32)
    ).astype(mixed_ref.dtype)


def mix(amplitudes, after):
    pairs, width, _ = amplitudes.shape
    spec = pl.BlockSpec((1, width, width), lambda p: (p, 0, 0))
    return pl.pallas_call(
        mix_kernel,
        grid=(pairs,),
        out_shape=jax.ShapeDtypeStruct(amplitudes.shape, amplitudes.dtype),
        in_specs=[spec, ANY],
        out_specs=spec,
        cost_estimate=pl.CostEstimate(
            flops=pairs * width * width, bytes_accessed=4 * pairs * width * width, transcendentals=0
        ),
        compiler_params=pltpu.CompilerParams(vmem_limit_bytes=BIG),
        name="mix_amplitudes",
    )(amplitudes, after)


def residual_kernel(
    rows_first, tile, place_ref, occ_ref, domain_ref, eps_occ_ref, eps_vir_ref,
    mixed_ref, first_ref, second_ref, out_ref, block, sem,
):
    pair = pl.program_id(0)
    pairs = pl.num_programs(0)
    width = out_ref.shape[2]
    count = width // tile

    def fetch(which):
        slot = which % 2

        def step(k, carry):
            row = pl.multiple_of((k // count) * tile, tile)
            column = pl.ds(pl.multiple_of((k % count) * tile, tile), tile)
            place = place_ref[which * count * count + k]
            pltpu.make_async_copy(
                first_ref.at[place], block.at[slot, pl.ds(row, rows_first), column], sem.at[slot]
            ).start()
            pltpu.make_async_copy(
                second_ref.at[place],
                block.at[slot, pl.ds(row + rows_first, tile - rows_first), column],
                sem.at[slot],
            ).start()
            return carry

        lax.fori_loop(0, count * count, step, 0)

    @pl.when(pair == 0)
    def _():
        fetch(0)

    @pl.when(pair + 1 < pairs)
    def _():
        fetch(pair + 1)

    now = pair % 2
    pltpu.make_async_copy(block.at[now], block.at[now], sem.at[now]).wait()

    occ = eps_occ_ref[occ_ref[2 * pair]] + eps_occ_ref[occ_ref[2 * pair + 1]]
    energies = [
        eps_vir_ref[pl.ds(domain_ref[count * pair + c], 1), :] for c in range(count)
    ]
    across = jnp.concatenate(energies, axis=1)
    for c in range(0, count, 2):
        part = pl.ds(c * tile, 2 * tile)
        down = jnp.transpose(
            jnp.broadcast_to(jnp.concatenate(energies[c : c + 2], axis=1), (8, 2 * tile))
        )[:, :1]
        total = jnp.dot(
            mixed_ref[0, part, :], block[now], preferred_element_type=jnp.float32
        )
        total = total + lax.dot_general(
            block[now, :, part],
            mixed_ref[0],
            (((0,), (0,)), ((), ())),
            preferred_element_type=jnp.float32,
        )
        out_ref[0, part, :] = total / (occ - down - across)


def residual(places, pair_occ, domain, eps_occ, eps_vir, mixed, first, second):
    pairs, width, _ = mixed.shape
    rows_first, tile = first.shape[1], first.shape[2]
    return pl.pallas_call(
        functools.partial(residual_kernel, rows_first, tile),
        grid=(pairs,),
        out_shape=jax.ShapeDtypeStruct(mixed.shape, jnp.float32),
        in_specs=[
            SMEM,
            SMEM,
            SMEM,
            SMEM,
            pl.BlockSpec(memory_space=pltpu.VMEM),
            pl.BlockSpec((1, width, width), lambda p: (p, 0, 0)),
            ANY,
            ANY,
        ],
        out_specs=pl.BlockSpec((1, width, width), lambda p: (p, 0, 0)),
        scratch_shapes=[
            pltpu.VMEM((2, width, width), mixed.dtype),
            pltpu.SemaphoreType.DMA((2,)),
        ],
        cost_estimate=pl.CostEstimate(
            flops=4 * pairs * width**3, bytes_accessed=8 * pairs * width**2, transcendentals=0
        ),
        compiler_params=pltpu.CompilerParams(vmem_limit_bytes=BIG),
        name="residual",
    )(places, pair_occ, domain, eps_occ, eps_vir, mixed, first, second)


def body(amplitudes, integral_tiles, need_owner, need_slot, pair_occ, domain, eps_occ, eps_vir):
    held, tile, _ = integral_tiles.shape
    vir = lax.axis_size("vir")
    here = lax.axis_index("pair").astype(jnp.int32).reshape(1)
    near = from_others(integral_tiles[:, :ROWS_FIRST])
    gathered = lax.all_gather(integral_tiles[:, ROWS_FIRST:], "pair", axis=0, tiled=True)
    requests, places = ask(need_owner.reshape(1, -1), need_slot.reshape(1, -1), vir, held)
    codes = lax.all_to_all(
        requests.reshape(vir, 1, PER_COLUMN), "vir", split_axis=0, concat_axis=0, tiled=True
    )

    served = serve(here, codes, integral_tiles, near, 0, ROWS_FIRST)
    mixed = mix(amplitudes, served)
    got_first = lax.all_to_all(served, "vir", split_axis=0, concat_axis=0, tiled=True)
    served = serve_gathered(codes, gathered)
    got_second = lax.all_to_all(served, "vir", split_axis=0, concat_axis=0, tiled=True)
    return residual(
        places.reshape(-1),
        pair_occ.reshape(-1),
        domain.reshape(-1),
        eps_occ,
        eps_vir.reshape(-1, tile),
        mixed,
        got_first,
        got_second,
    )


def solution(mesh):
    split_both = ("pair", "vir")
    return jax.shard_map(
        body,
        mesh=mesh,
        in_specs=(
            P(split_both, None, None),
            P(split_both, None, None),
            P(split_both, None),
            P(split_both, None),
            P(split_both, None),
            P(split_both, None),
            P(),
            P(),
        ),
        out_specs=P(split_both, None, None),
        check_vma=False,
    )
```

```python
import functools

import jax
import jax.numpy as jnp
from jax import lax
from jax.experimental import pallas as pl
from jax.experimental.pallas import tpu as pltpu
from jax.sharding import PartitionSpec as P

ROWS_FIRST = 48
PER_COLUMN = 3
ANY = pl.BlockSpec(memory_space=pl.ANY)
VMEM = pl.BlockSpec(memory_space=pltpu.VMEM)
SMEM = pl.BlockSpec(memory_space=pltpu.SMEM)
BIG = 100 * 2**20 // 2


def ask_kernel(held, owner_ref, slot_ref, request_ref, place_ref):
    vir = request_ref.shape[0]
    owner, slot = owner_ref[...], slot_ref[...]
    asks = owner.shape[1]
    column = owner % vir
    code = (owner // vir) * held + slot
    along = jnp.broadcast_to(column, (asks, asks))
    down = jnp.transpose(along)
    at_row = lax.broadcasted_iota(jnp.int32, (asks, asks), 0)
    at_column = lax.broadcasted_iota(jnp.int32, (asks, asks), 1)
    earlier = jnp.where((along == down) & (at_row < at_column), 1, 0)
    place = column * PER_COLUMN + jnp.sum(earlier, axis=0, keepdims=True)
    place_ref[...] = place
    target = lax.broadcasted_iota(jnp.int32, (vir, asks), 0) * PER_COLUMN
    request_ref[...] = jnp.concatenate(
        [
            jnp.sum(jnp.where(place == target + k, code, 0), axis=1, keepdims=True)
            for k in range(PER_COLUMN)
        ],
        axis=1,
    )


def ask(owner, slot, vir, held):
    return pl.pallas_call(
        functools.partial(ask_kernel, held),
        out_shape=(
            jax.ShapeDtypeStruct((vir, PER_COLUMN), jnp.int32),
            jax.ShapeDtypeStruct(owner.shape, jnp.int32),
        ),
        in_specs=[VMEM, VMEM],
        out_specs=(VMEM, VMEM),
        name="make_requests",
    )(owner, slot)


def serve_kernel(n_pair, here_ref, code_ref, *refs):
    sources, (out_ref, pool, sem) = refs[:n_pair], refs[n_pair:]
    held = sources[0].shape[0]
    copies = []
    for step in range(n_pair):
        owner = (here_ref[0] + step) % n_pair
        target = pool.at[pl.ds(owner * held, held)]
        copies.append(pltpu.make_async_copy(sources[step], target, sem.at[step]))
    for copy in copies:
        copy.start()
    for copy in copies:
        copy.wait()
    take(code_ref, pool, out_ref)


def take(code_ref, pool, out_ref):
    def step(column, carry):
        for k in range(PER_COLUMN):
            out_ref[column * PER_COLUMN + k] = pool[code_ref[column, 0, k]]
        return carry

    lax.fori_loop(0, code_ref.shape[0], step, 0, unroll=4)


def serve(here, codes, sources):
    slots = codes.shape[0] * PER_COLUMN
    n_pair = len(sources)
    held, rows, tile = sources[0].shape
    dtype = sources[0].dtype
    return pl.pallas_call(
        functools.partial(serve_kernel, n_pair),
        out_shape=jax.ShapeDtypeStruct((slots, rows, tile), dtype),
        in_specs=[SMEM, SMEM] + [ANY] * n_pair,
        out_specs=VMEM,
        scratch_shapes=[
            pltpu.VMEM((n_pair * held, rows, tile), dtype),
            pltpu.SemaphoreType.DMA((n_pair,)),
        ],
        compiler_params=pltpu.CompilerParams(vmem_limit_bytes=BIG),
        cost_estimate=pl.CostEstimate(
            flops=0, bytes_accessed=4 * slots * rows * tile, transcendentals=0
        ),
        name="serve_tiles",
    )(here, codes, *sources)


def cut_kernel(row_from, tiles_ref, after_ref, out_ref, sem):
    copy = pltpu.make_async_copy(
        tiles_ref.at[:, pl.ds(row_from, out_ref.shape[1])], out_ref, sem
    )
    copy.start()
    copy.wait()


def cut(tiles, after, row_from, rows):
    held, _, tile = tiles.shape
    return pl.pallas_call(
        functools.partial(cut_kernel, row_from),
        out_shape=jax.ShapeDtypeStruct((held, rows, tile), tiles.dtype),
        in_specs=[ANY, ANY],
        out_specs=VMEM,
        scratch_shapes=[pltpu.SemaphoreType.DMA],
        compiler_params=pltpu.CompilerParams(vmem_limit_bytes=BIG),
        cost_estimate=pl.CostEstimate(
            flops=0, bytes_accessed=4 * held * rows * tile, transcendentals=0
        ),
        name="cut_rows",
    )(tiles, after)


def from_others(mine):
    n = lax.axis_size("pair")
    return [mine] + [
        lax.ppermute(mine, "pair", [((i + step) % n, i) for i in range(n)])
        for step in range(1, n)
    ]


def mix_kernel(amp_ref, after_ref, mixed_ref):
    amp = amp_ref[0]
    mixed_ref[0] = (
        2.0 * amp.astype(jnp.float32) - jnp.transpose(amp).astype(jnp.float32)
    ).astype(mixed_ref.dtype)


def mix(amplitudes, after):
    pairs, width, _ = amplitudes.shape
    spec = pl.BlockSpec((1, width, width), lambda p: (p, 0, 0))
    return pl.pallas_call(
        mix_kernel,
        grid=(pairs,),
        out_shape=jax.ShapeDtypeStruct(amplitudes.shape, amplitudes.dtype),
        in_specs=[spec, ANY],
        out_specs=spec,
        cost_estimate=pl.CostEstimate(
            flops=pairs * width * width, bytes_accessed=4 * pairs * width * width, transcendentals=0
        ),
        compiler_params=pltpu.CompilerParams(vmem_limit_bytes=BIG),
        name="mix_amplitudes",
    )(amplitudes, after)


def residual_kernel(
    rows_first, tile, place_ref, occ_ref, domain_ref, eps_occ_ref, eps_vir_ref,
    mixed_ref, first_ref, second_ref, out_ref, block, sem,
):
    pair = pl.program_id(0)
    pairs = pl.num_programs(0)
    width = out_ref.shape[2]
    count = width // tile

    def fetch(which):
        slot = which % 2

        def step(k, carry):
            row = pl.multiple_of((k // count) * tile, tile)
            column = pl.ds(pl.multiple_of((k % count) * tile, tile), tile)
            place = place_ref[which * count * count + k]
            pltpu.make_async_copy(
                first_ref.at[place], block.at[slot, pl.ds(row, rows_first), column], sem.at[slot]
            ).start()
            pltpu.make_async_copy(
                second_ref.at[place],
                block.at[slot, pl.ds(row + rows_first, tile - rows_first), column],
                sem.at[slot],
            ).start()
            return carry

        lax.fori_loop(0, count * count, step, 0)

    @pl.when(pair == 0)
    def _():
        fetch(0)

    @pl.when(pair + 1 < pairs)
    def _():
        fetch(pair + 1)

    now = pair % 2
    pltpu.make_async_copy(block.at[now], block.at[now], sem.at[now]).wait()

    occ = eps_occ_ref[occ_ref[2 * pair]] + eps_occ_ref[occ_ref[2 * pair + 1]]
    energies = [
        eps_vir_ref[pl.ds(domain_ref[count * pair + c], 1), :] for c in range(count)
    ]
    across = jnp.concatenate(energies, axis=1)
    for c in range(0, count, 2):
        part = pl.ds(c * tile, 2 * tile)
        down = jnp.transpose(
            jnp.broadcast_to(jnp.concatenate(energies[c : c + 2], axis=1), (8, 2 * tile))
        )[:, :1]
        total = jnp.dot(
            mixed_ref[0, part, :], block[now], preferred_element_type=jnp.float32
        )
        total = total + lax.dot_general(
            block[now, :, part],
            mixed_ref[0],
            (((0,), (0,)), ((), ())),
            preferred_element_type=jnp.float32,
        )
        out_ref[0, part, :] = total / (occ - down - across)


def residual(places, pair_occ, domain, eps_occ, eps_vir, mixed, first, second):
    pairs, width, _ = mixed.shape
    rows_first, tile = first.shape[1], first.shape[2]
    return pl.pallas_call(
        functools.partial(residual_kernel, rows_first, tile),
        grid=(pairs,),
        out_shape=jax.ShapeDtypeStruct(mixed.shape, jnp.float32),
        in_specs=[
            SMEM,
            SMEM,
            SMEM,
            SMEM,
            pl.BlockSpec(memory_space=pltpu.VMEM),
            pl.BlockSpec((1, width, width), lambda p: (p, 0, 0)),
            ANY,
            ANY,
        ],
        out_specs=pl.BlockSpec((1, width, width), lambda p: (p, 0, 0)),
        scratch_shapes=[
            pltpu.VMEM((2, width, width), mixed.dtype),
            pltpu.SemaphoreType.DMA((2,)),
        ],
        cost_estimate=pl.CostEstimate(
            flops=4 * pairs * width**3, bytes_accessed=8 * pairs * width**2, transcendentals=0
        ),
        compiler_params=pltpu.CompilerParams(vmem_limit_bytes=BIG),
        name="residual",
    )(places, pair_occ, domain, eps_occ, eps_vir, mixed, first, second)


def body(amplitudes, integral_tiles, need_owner, need_slot, pair_occ, domain, eps_occ, eps_vir):
    held, tile, _ = integral_tiles.shape
    vir = lax.axis_size("vir")
    here = lax.axis_index("pair").astype(jnp.int32).reshape(1)
    near = from_others(integral_tiles[:, :ROWS_FIRST])
    rest = tile - ROWS_FIRST
    far = from_others(cut(integral_tiles, near[1], ROWS_FIRST, rest))
    requests, places = ask(need_owner.reshape(1, -1), need_slot.reshape(1, -1), vir, held)
    codes = lax.all_to_all(
        requests.reshape(vir, 1, PER_COLUMN), "vir", split_axis=0, concat_axis=0, tiled=True
    )

    served = serve(here, codes, near)
    mixed = mix(amplitudes, codes)
    got_first = lax.all_to_all(served, "vir", split_axis=0, concat_axis=0, tiled=True)
    served = serve(here, codes, far)
    got_second = lax.all_to_all(served, "vir", split_axis=0, concat_axis=0, tiled=True)
    return residual(
        places.reshape(-1),
        pair_occ.reshape(-1),
        domain.reshape(-1),
        eps_occ,
        eps_vir.reshape(-1, tile),
        mixed,
        got_first,
        got_second,
    )


def solution(mesh):
    split_both = ("pair", "vir")
    return jax.shard_map(
        body,
        mesh=mesh,
        in_specs=(
            P(split_both, None, None),
            P(split_both, None, None),
            P(split_both, None),
            P(split_both, None),
            P(split_both, None),
            P(split_both, None),
            P(),
            P(),
        ),
        out_specs=P(split_both, None, None),
        check_vma=False,
    )
```

```python
import functools

import jax
import jax.numpy as jnp
from jax import lax
from jax.experimental import pallas as pl
from jax.experimental.pallas import tpu as pltpu
from jax.sharding import PartitionSpec as P

ROWS_FIRST = 32
PER_COLUMN = 3
LONG = 400_000_000_000
ANY = pl.BlockSpec(memory_space=pl.ANY)
VMEM = pl.BlockSpec(memory_space=pltpu.VMEM)
SMEM = pl.BlockSpec(memory_space=pltpu.SMEM)
BIG = 100 * 2**20 // 2


def ask_kernel(held, owner_ref, slot_ref, tiles_ref, request_ref, place_ref, first_ref, rest_ref, sem):
    vir = request_ref.shape[0]
    rows = first_ref.shape[1]
    copies = [
        pltpu.make_async_copy(tiles_ref.at[:, pl.ds(0, rows)], first_ref, sem.at[0]),
        pltpu.make_async_copy(
            tiles_ref.at[:, pl.ds(rows, rest_ref.shape[1])], rest_ref, sem.at[1]
        ),
    ]
    for copy in copies:
        copy.start()
    owner, slot = owner_ref[...], slot_ref[...]
    asks = owner.shape[1]
    column = owner % vir
    code = (owner // vir) * held + slot
    along = jnp.broadcast_to(column, (asks, asks))
    down = jnp.transpose(along)
    at_row = lax.broadcasted_iota(jnp.int32, (asks, asks), 0)
    at_column = lax.broadcasted_iota(jnp.int32, (asks, asks), 1)
    earlier = jnp.where((along == down) & (at_row < at_column), 1, 0)
    place = column * PER_COLUMN + jnp.sum(earlier, axis=0, keepdims=True)
    place_ref[...] = place
    target = lax.broadcasted_iota(jnp.int32, (vir, asks), 0) * PER_COLUMN
    request_ref[...] = jnp.concatenate(
        [
            jnp.sum(jnp.where(place == target + k, code, 0), axis=1, keepdims=True)
            for k in range(PER_COLUMN)
        ],
        axis=1,
    )
    for copy in copies:
        copy.wait()


def ask(owner, slot, tiles, vir):
    held, _, tile = tiles.shape
    return pl.pallas_call(
        functools.partial(ask_kernel, held),
        out_shape=(
            jax.ShapeDtypeStruct((vir, PER_COLUMN), jnp.int32),
            jax.ShapeDtypeStruct(owner.shape, jnp.int32),
            jax.ShapeDtypeStruct((held, ROWS_FIRST, tile), tiles.dtype),
            jax.ShapeDtypeStruct((held, tile - ROWS_FIRST, tile), tiles.dtype),
        ),
        in_specs=[VMEM, VMEM, ANY],
        out_specs=(VMEM, VMEM, VMEM, VMEM),
        scratch_shapes=[pltpu.SemaphoreType.DMA((2,))],
        name="make_requests",
    )(owner, slot, tiles)


def fill_pool(n_pair, held, parts, here_ref, sources, pool, sem):
    copies = []
    for k, (step, start) in enumerate(parts):
        owner = (here_ref[0] + step) % n_pair
        target = pool.at[pl.ds(owner * held + start, sources[k].shape[0])]
        copies.append(pltpu.make_async_copy(sources[k], target, sem.at[k]))
    for copy in copies:
        copy.start()
    for copy in copies:
        copy.wait()


def pool_kernel(n_pair, held, parts, here_ref, after_ref, rest_ref, *refs):
    sources, (pool, passed_ref, sem) = refs[: len(parts)], refs[len(parts) :]
    fill_pool(n_pair, held, parts, here_ref, sources, pool, sem)


def pool_first(here, after, rest, parts, n_pair, held):
    sources = [source for _, _, source in parts]
    _, rows, tile = sources[0].shape
    return pl.pallas_call(
        functools.partial(pool_kernel, n_pair, held, [part[:2] for part in parts]),
        out_shape=(
            jax.ShapeDtypeStruct((n_pair * held, rows, tile), rest.dtype),
            jax.ShapeDtypeStruct(rest.shape, rest.dtype),
        ),
        in_specs=[SMEM, ANY, ANY] + [ANY] * len(parts),
        out_specs=(VMEM, ANY),
        scratch_shapes=[pltpu.SemaphoreType.DMA((len(parts),))],
        input_output_aliases={2: 1},
        compiler_params=pltpu.CompilerParams(vmem_limit_bytes=BIG),
        name="pool_tiles",
    )(here, after, rest, *sources)


def serve_kernel(n_pair, held, parts, here_ref, code_ref, *refs):
    sources, (out_ref, pool, sem) = refs[: len(parts)], refs[len(parts) :]
    fill_pool(n_pair, held, parts, here_ref, sources, pool, sem)
    take(code_ref, pool, out_ref)


def serve_pool(codes, pool):
    slots = codes.shape[0] * PER_COLUMN
    _, rows, tile = pool.shape
    return pl.pallas_call(
        take,
        out_shape=jax.ShapeDtypeStruct((slots, rows, tile), pool.dtype),
        in_specs=[SMEM, VMEM],
        out_specs=VMEM,
        compiler_params=pltpu.CompilerParams(vmem_limit_bytes=BIG),
        cost_estimate=pl.CostEstimate(
            flops=0, bytes_accessed=4 * slots * rows * tile, transcendentals=0
        ),
        name="serve_pool",
    )(codes, pool)


def take(code_ref, pool, out_ref):
    def step(column, carry):
        for k in range(PER_COLUMN):
            out_ref[column * PER_COLUMN + k] = pool[code_ref[column, 0, k]]
        return carry

    lax.fori_loop(0, code_ref.shape[0], step, 0, unroll=4)


def serve(here, codes, parts, n_pair, held):
    slots = codes.shape[0] * PER_COLUMN
    sources = [source for _, _, source in parts]
    _, rows, tile = sources[0].shape
    dtype = sources[0].dtype
    return pl.pallas_call(
        functools.partial(serve_kernel, n_pair, held, [part[:2] for part in parts]),
        out_shape=jax.ShapeDtypeStruct((slots, rows, tile), dtype),
        in_specs=[SMEM, SMEM] + [ANY] * len(parts),
        out_specs=VMEM,
        scratch_shapes=[
            pltpu.VMEM((n_pair * held, rows, tile), dtype),
            pltpu.SemaphoreType.DMA((len(parts),)),
        ],
        compiler_params=pltpu.CompilerParams(vmem_limit_bytes=BIG),
        cost_estimate=pl.CostEstimate(
            flops=0, bytes_accessed=4 * slots * rows * tile, transcendentals=0
        ),
        name="serve_tiles",
    )(here, codes, *sources)


def halves_kernel(up_ref, down_ref, low_ref, high_ref, sem):
    half = low_ref.shape[0]
    first = pltpu.make_async_copy(up_ref.at[pl.ds(0, half)], low_ref, sem.at[0])
    second = pltpu.make_async_copy(down_ref.at[pl.ds(half, half)], high_ref, sem.at[1])
    first.start()
    second.start()
    first.wait()
    second.wait()


def halves(up, down):
    held, rows, tile = up.shape
    shape = jax.ShapeDtypeStruct((held // 2, rows, tile), up.dtype)
    return pl.pallas_call(
        halves_kernel,
        out_shape=(shape, shape),
        in_specs=[ANY, ANY],
        out_specs=(VMEM, VMEM),
        scratch_shapes=[pltpu.SemaphoreType.DMA((2,))],
        compiler_params=pltpu.CompilerParams(vmem_limit_bytes=BIG),
        cost_estimate=pl.CostEstimate(
            flops=LONG, bytes_accessed=0, transcendentals=0
        ),
        name="cut_halves",
    )(up, down)


def from_others(mine):
    n = lax.axis_size("pair")
    return [(0, 0, mine)] + [
        (step, 0, lax.ppermute(mine, "pair", [((i + step) % n, i) for i in range(n)]))
        for step in range(1, n)
    ]


def from_ring(mine):
    n = lax.axis_size("pair")
    up = [(i, (i + 1) % n) for i in range(n)]
    down = [(i, (i + n - 1) % n) for i in range(n)]
    below = lax.ppermute(mine, "pair", up)
    above = lax.ppermute(mine, "pair", down)
    low, high = halves(below, above)
    far_low = lax.ppermute(low, "pair", up)
    far_high = lax.ppermute(high, "pair", down)
    half = mine.shape[0] // 2
    return [(0, 0, mine), (1, 0, above), (3, 0, below), (2, 0, far_low), (2, half, far_high)]


def mix_kernel(amp_ref, after_ref, mixed_ref):
    amp = amp_ref[0]
    mixed_ref[0] = (
        2.0 * amp.astype(jnp.float32) - jnp.transpose(amp).astype(jnp.float32)
    ).astype(mixed_ref.dtype)


def mix(amplitudes, after):
    pairs, width, _ = amplitudes.shape
    spec = pl.BlockSpec((1, width, width), lambda p: (p, 0, 0))
    return pl.pallas_call(
        mix_kernel,
        grid=(pairs,),
        out_shape=jax.ShapeDtypeStruct(amplitudes.shape, amplitudes.dtype),
        in_specs=[spec, ANY],
        out_specs=spec,
        cost_estimate=pl.CostEstimate(
            flops=pairs * width * width, bytes_accessed=4 * pairs * width * width, transcendentals=0
        ),
        compiler_params=pltpu.CompilerParams(vmem_limit_bytes=BIG),
        name="mix_amplitudes",
    )(amplitudes, after)


def residual_kernel(
    rows_first, tile, place_ref, occ_ref, domain_ref, eps_occ_ref, eps_vir_ref,
    mixed_ref, first_ref, second_ref, out_ref, block, sem,
):
    pair = pl.program_id(0)
    pairs = pl.num_programs(0)
    width = out_ref.shape[2]
    count = width // tile

    def fetch(which):
        slot = which % 2

        for k in range(count * count):
            row, column = k // count * tile, pl.ds(k % count * tile, tile)
            place = place_ref[which * count * count + k]
            pltpu.make_async_copy(
                first_ref.at[place], block.at[slot, pl.ds(row, rows_first), column], sem.at[slot]
            ).start()
            pltpu.make_async_copy(
                second_ref.at[place],
                block.at[slot, pl.ds(row + rows_first, tile - rows_first), column],
                sem.at[slot],
            ).start()

    @pl.when(pair == 0)
    def _():
        fetch(0)

    @pl.when(pair + 1 < pairs)
    def _():
        fetch(pair + 1)

    now = pair % 2
    pltpu.make_async_copy(block.at[now], block.at[now], sem.at[now]).wait()

    occ = eps_occ_ref[occ_ref[2 * pair]] + eps_occ_ref[occ_ref[2 * pair + 1]]
    energies = [
        eps_vir_ref[pl.ds(domain_ref[count * pair + c], 1), :] for c in range(count)
    ]
    across = jnp.concatenate(energies, axis=1)
    for c in range(0, count, 2):
        part = pl.ds(c * tile, 2 * tile)
        down = jnp.transpose(
            jnp.broadcast_to(jnp.concatenate(energies[c : c + 2], axis=1), (8, 2 * tile))
        )[:, :1]
        total = jnp.dot(
            mixed_ref[0, part, :], block[now], preferred_element_type=jnp.float32
        )
        total = total + lax.dot_general(
            block[now, :, part],
            mixed_ref[0],
            (((0,), (0,)), ((), ())),
            preferred_element_type=jnp.float32,
        )
        out_ref[0, part, :] = total / (occ - down - across)


def residual(places, pair_occ, domain, eps_occ, eps_vir, mixed, first, second):
    pairs, width, _ = mixed.shape
    rows_first, tile = first.shape[1], first.shape[2]
    return pl.pallas_call(
        functools.partial(residual_kernel, rows_first, tile),
        grid=(pairs,),
        out_shape=jax.ShapeDtypeStruct(mixed.shape, jnp.float32),
        in_specs=[
            SMEM,
            SMEM,
            SMEM,
            SMEM,
            pl.BlockSpec(memory_space=pltpu.VMEM),
            pl.BlockSpec((1, width, width), lambda p: (p, 0, 0)),
            ANY,
            ANY,
        ],
        out_specs=pl.BlockSpec((1, width, width), lambda p: (p, 0, 0)),
        scratch_shapes=[
            pltpu.VMEM((2, width, width), mixed.dtype),
            pltpu.SemaphoreType.DMA((2,)),
        ],
        cost_estimate=pl.CostEstimate(
            flops=4 * pairs * width**3, bytes_accessed=8 * pairs * width**2, transcendentals=0
        ),
        compiler_params=pltpu.CompilerParams(vmem_limit_bytes=BIG),
        name="residual",
    )(places, pair_occ, domain, eps_occ, eps_vir, mixed, first, second)


def body(amplitudes, integral_tiles, need_owner, need_slot, pair_occ, domain, eps_occ, eps_vir):
    held = integral_tiles.shape[0]
    tile = integral_tiles.shape[1]
    vir = lax.axis_size("vir")
    here = lax.axis_index("pair").astype(jnp.int32).reshape(1)
    n_pair = lax.axis_size("pair")
    requests, places, first, rest = ask(
        need_owner.reshape(1, -1), need_slot.reshape(1, -1), integral_tiles, vir
    )
    near = from_others(first)
    codes = lax.all_to_all(
        requests.reshape(vir, 1, PER_COLUMN), "vir", split_axis=0, concat_axis=0, tiled=True
    )
    pool, rest = pool_first(here, codes, rest, near, n_pair, held)
    far = from_ring(rest)
    mixed = mix(amplitudes, codes)
    served = serve_pool(codes, pool)
    got_first = lax.all_to_all(served, "vir", split_axis=0, concat_axis=0, tiled=True)
    served = serve(here, codes, far, n_pair, held)
    got_second = lax.all_to_all(served, "vir", split_axis=0, concat_axis=0, tiled=True)
    return residual(
        places.reshape(-1),
        pair_occ.reshape(-1),
        domain.reshape(-1),
        eps_occ,
        eps_vir.reshape(-1, tile),
        mixed,
        got_first,
        got_second,
    )


def solution(mesh):
    split_both = ("pair", "vir")
    return jax.shard_map(
        body,
        mesh=mesh,
        in_specs=(
            P(split_both, None, None),
            P(split_both, None, None),
            P(split_both, None),
            P(split_both, None),
            P(split_both, None),
            P(split_both, None),
            P(),
            P(),
        ),
        out_specs=P(split_both, None, None),
        check_vma=False,
    )
```

```python
import functools

import jax
import jax.numpy as jnp
from jax import lax
from jax.experimental import pallas as pl
from jax.experimental.pallas import tpu as pltpu
from jax.sharding import PartitionSpec as P

ROWS_FIRST = 32
PER_COLUMN = 3
LONG = 400_000_000_000
ANY = pl.BlockSpec(memory_space=pl.ANY)
VMEM = pl.BlockSpec(memory_space=pltpu.VMEM)
SMEM = pl.BlockSpec(memory_space=pltpu.SMEM)
BIG = 100 * 2**20 // 2


def ask_kernel(held, owner_ref, slot_ref, tiles_ref, request_ref, place_ref, first_ref, sem):
    vir = request_ref.shape[0]
    copy = pltpu.make_async_copy(
        tiles_ref.at[:, pl.ds(0, first_ref.shape[1])], first_ref, sem
    )
    copy.start()
    owner, slot = owner_ref[...], slot_ref[...]
    asks = owner.shape[1]
    column = owner % vir
    code = (owner // vir) * held + slot
    along = jnp.broadcast_to(column, (asks, asks))
    down = jnp.transpose(along)
    at_row = lax.broadcasted_iota(jnp.int32, (asks, asks), 0)
    at_column = lax.broadcasted_iota(jnp.int32, (asks, asks), 1)
    earlier = jnp.where((along == down) & (at_row < at_column), 1, 0)
    place = column * PER_COLUMN + jnp.sum(earlier, axis=0, keepdims=True)
    place_ref[...] = place
    target = lax.broadcasted_iota(jnp.int32, (vir, asks), 0) * PER_COLUMN
    request_ref[...] = jnp.concatenate(
        [
            jnp.sum(jnp.where(place == target + k, code, 0), axis=1, keepdims=True)
            for k in range(PER_COLUMN)
        ],
        axis=1,
    )
    copy.wait()


def ask(owner, slot, tiles, vir):
    held, _, tile = tiles.shape
    return pl.pallas_call(
        functools.partial(ask_kernel, held),
        out_shape=(
            jax.ShapeDtypeStruct((vir, PER_COLUMN), jnp.int32),
            jax.ShapeDtypeStruct(owner.shape, jnp.int32),
            jax.ShapeDtypeStruct((held, ROWS_FIRST, tile), tiles.dtype),
        ),
        in_specs=[VMEM, VMEM, ANY],
        out_specs=(VMEM, VMEM, VMEM),
        scratch_shapes=[pltpu.SemaphoreType.DMA],
        name="make_requests",
    )(owner, slot, tiles)


def fill_pool(n_pair, held, parts, here_ref, sources, pool, sem):
    copies = []
    for k, (step, start) in enumerate(parts):
        owner = (here_ref[0] + step) % n_pair
        target = pool.at[pl.ds(owner * held + start, sources[k].shape[0])]
        copies.append(pltpu.make_async_copy(sources[k], target, sem.at[k]))
    for copy in copies:
        copy.start()
    for copy in copies:
        copy.wait()


def gate_kernel(rows_ref, code_ref, sample_ref, out_ref):
    pass


def gate(rows, codes, sample):
    return pl.pallas_call(
        gate_kernel,
        out_shape=jax.ShapeDtypeStruct(rows.shape, rows.dtype),
        in_specs=[ANY, ANY, ANY],
        out_specs=ANY,
        input_output_aliases={0: 0},
        name="gate_rows",
    )(rows, codes, sample)


def serve_kernel(n_pair, held, parts, here_ref, code_ref, *refs):
    sources, (out_ref, pool, sem) = refs[: len(parts)], refs[len(parts) :]
    fill_pool(n_pair, held, parts, here_ref, sources, pool, sem)
    take(code_ref, pool, out_ref)


def take(code_ref, pool, out_ref):
    def step(column, carry):
        for k in range(PER_COLUMN):
            out_ref[column * PER_COLUMN + k] = pool[code_ref[column, 0, k]]
        return carry

    lax.fori_loop(0, code_ref.shape[0], step, 0, unroll=4)


def serve(here, codes, parts, n_pair, held):
    slots = codes.shape[0] * PER_COLUMN
    sources = [source for _, _, source in parts]
    _, rows, tile = sources[0].shape
    dtype = sources[0].dtype
    return pl.pallas_call(
        functools.partial(serve_kernel, n_pair, held, [part[:2] for part in parts]),
        out_shape=jax.ShapeDtypeStruct((slots, rows, tile), dtype),
        in_specs=[SMEM, SMEM] + [ANY] * len(parts),
        out_specs=VMEM,
        scratch_shapes=[
            pltpu.VMEM((n_pair * held, rows, tile), dtype),
            pltpu.SemaphoreType.DMA((len(parts),)),
        ],
        compiler_params=pltpu.CompilerParams(vmem_limit_bytes=BIG),
        cost_estimate=pl.CostEstimate(
            flops=0, bytes_accessed=4 * slots * rows * tile, transcendentals=0
        ),
        name="serve_tiles",
    )(here, codes, *sources)


def halves_kernel(up_ref, down_ref, low_ref, high_ref, sem):
    half = low_ref.shape[0]
    first = pltpu.make_async_copy(up_ref.at[pl.ds(0, half)], low_ref, sem.at[0])
    second = pltpu.make_async_copy(down_ref.at[pl.ds(half, half)], high_ref, sem.at[1])
    first.start()
    second.start()
    first.wait()
    second.wait()


def halves(up, down):
    held, rows, tile = up.shape
    shape = jax.ShapeDtypeStruct((held // 2, rows, tile), up.dtype)
    return pl.pallas_call(
        halves_kernel,
        out_shape=(shape, shape),
        in_specs=[ANY, ANY],
        out_specs=(VMEM, VMEM),
        scratch_shapes=[pltpu.SemaphoreType.DMA((2,))],
        compiler_params=pltpu.CompilerParams(vmem_limit_bytes=BIG),
        cost_estimate=pl.CostEstimate(
            flops=LONG, bytes_accessed=0, transcendentals=0
        ),
        name="cut_halves",
    )(up, down)


def from_others(mine):
    n = lax.axis_size("pair")
    return [(0, 0, mine)] + [
        (step, 0, lax.ppermute(mine, "pair", [((i + step) % n, i) for i in range(n)]))
        for step in range(1, n)
    ]


def from_ring(mine):
    n = lax.axis_size("pair")
    up = [(i, (i + 1) % n) for i in range(n)]
    down = [(i, (i + n - 1) % n) for i in range(n)]
    below = lax.ppermute(mine, "pair", up)
    above = lax.ppermute(mine, "pair", down)
    low, high = halves(below, above)
    far_low = lax.ppermute(low, "pair", up)
    far_high = lax.ppermute(high, "pair", down)
    half = mine.shape[0] // 2
    return [(0, 0, mine), (1, 0, above), (3, 0, below), (2, 0, far_low), (2, half, far_high)]


def mix_kernel(amp_ref, after_ref, mixed_ref):
    amp = amp_ref[0]
    mixed_ref[0] = (
        2.0 * amp.astype(jnp.float32) - jnp.transpose(amp).astype(jnp.float32)
    ).astype(mixed_ref.dtype)


def mix(amplitudes, after):
    pairs, width, _ = amplitudes.shape
    spec = pl.BlockSpec((1, width, width), lambda p: (p, 0, 0))
    return pl.pallas_call(
        mix_kernel,
        grid=(pairs,),
        out_shape=jax.ShapeDtypeStruct(amplitudes.shape, amplitudes.dtype),
        in_specs=[spec, ANY],
        out_specs=spec,
        cost_estimate=pl.CostEstimate(
            flops=pairs * width * width, bytes_accessed=4 * pairs * width * width, transcendentals=0
        ),
        compiler_params=pltpu.CompilerParams(vmem_limit_bytes=BIG),
        name="mix_amplitudes",
    )(amplitudes, after)


def residual_kernel(
    rows_first, tile, place_ref, occ_ref, domain_ref, eps_occ_ref, eps_vir_ref,
    mixed_ref, first_ref, second_ref, out_ref, block, sem,
):
    pair = pl.program_id(0)
    pairs = pl.num_programs(0)
    width = out_ref.shape[2]
    count = width // tile

    def fetch(which):
        slot = which % 2

        for k in range(count * count):
            row, column = k // count * tile, pl.ds(k % count * tile, tile)
            place = place_ref[which * count * count + k]
            pltpu.make_async_copy(
                first_ref.at[place], block.at[slot, pl.ds(row, rows_first), column], sem.at[slot]
            ).start()
            pltpu.make_async_copy(
                second_ref.at[place],
                block.at[slot, pl.ds(row + rows_first, tile - rows_first), column],
                sem.at[slot],
            ).start()

    @pl.when(pair == 0)
    def _():
        fetch(0)

    @pl.when(pair + 1 < pairs)
    def _():
        fetch(pair + 1)

    now = pair % 2
    pltpu.make_async_copy(block.at[now], block.at[now], sem.at[now]).wait()

    occ = eps_occ_ref[occ_ref[2 * pair]] + eps_occ_ref[occ_ref[2 * pair + 1]]
    energies = [
        eps_vir_ref[pl.ds(domain_ref[count * pair + c], 1), :] for c in range(count)
    ]
    across = jnp.concatenate(energies, axis=1)
    for c in range(0, count, 2):
        part = pl.ds(c * tile, 2 * tile)
        down = jnp.transpose(
            jnp.broadcast_to(jnp.concatenate(energies[c : c + 2], axis=1), (8, 2 * tile))
        )[:, :1]
        total = jnp.dot(
            mixed_ref[0, part, :], block[now], preferred_element_type=jnp.float32
        )
        total = total + lax.dot_general(
            block[now, :, part],
            mixed_ref[0],
            (((0,), (0,)), ((), ())),
            preferred_element_type=jnp.float32,
        )
        out_ref[0, part, :] = total / (occ - down - across)


def residual(places, pair_occ, domain, eps_occ, eps_vir, mixed, first, second):
    pairs, width, _ = mixed.shape
    rows_first, tile = first.shape[1], first.shape[2]
    return pl.pallas_call(
        functools.partial(residual_kernel, rows_first, tile),
        grid=(pairs,),
        out_shape=jax.ShapeDtypeStruct(mixed.shape, jnp.float32),
        in_specs=[
            SMEM,
            SMEM,
            SMEM,
            SMEM,
            pl.BlockSpec(memory_space=pltpu.VMEM),
            pl.BlockSpec((1, width, width), lambda p: (p, 0, 0)),
            ANY,
            ANY,
        ],
        out_specs=pl.BlockSpec((1, width, width), lambda p: (p, 0, 0)),
        scratch_shapes=[
            pltpu.VMEM((2, width, width), mixed.dtype),
            pltpu.SemaphoreType.DMA((2,)),
        ],
        cost_estimate=pl.CostEstimate(
            flops=4 * pairs * width**3, bytes_accessed=8 * pairs * width**2, transcendentals=0
        ),
        compiler_params=pltpu.CompilerParams(vmem_limit_bytes=BIG),
        name="residual",
    )(places, pair_occ, domain, eps_occ, eps_vir, mixed, first, second)


def body(amplitudes, integral_tiles, need_owner, need_slot, pair_occ, domain, eps_occ, eps_vir):
    held = integral_tiles.shape[0]
    tile = integral_tiles.shape[1]
    vir = lax.axis_size("vir")
    here = lax.axis_index("pair").astype(jnp.int32).reshape(1)
    n_pair = lax.axis_size("pair")
    requests, places, first = ask(
        need_owner.reshape(1, -1), need_slot.reshape(1, -1), integral_tiles, vir
    )
    near = from_others(first)
    codes = lax.all_to_all(
        requests.reshape(vir, 1, PER_COLUMN), "vir", split_axis=0, concat_axis=0, tiled=True
    )
    sample = sum(part[0, :8] for _, _, part in near[1:])
    far = from_ring(gate(integral_tiles[:, ROWS_FIRST:], codes, sample))
    mixed = mix(amplitudes, codes)
    served = serve(here, codes, near, n_pair, held)
    got_first = lax.all_to_all(served, "vir", split_axis=0, concat_axis=0, tiled=True)
    served = serve(here, codes, far, n_pair, held)
    got_second = lax.all_to_all(served, "vir", split_axis=0, concat_axis=0, tiled=True)
    return residual(
        places.reshape(-1),
        pair_occ.reshape(-1),
        domain.reshape(-1),
        eps_occ,
        eps_vir.reshape(-1, tile),
        mixed,
        got_first,
        got_second,
    )


def solution(mesh):
    split_both = ("pair", "vir")
    return jax.shard_map(
        body,
        mesh=mesh,
        in_specs=(
            P(split_both, None, None),
            P(split_both, None, None),
            P(split_both, None),
            P(split_both, None),
            P(split_both, None),
            P(split_both, None),
            P(),
            P(),
        ),
        out_specs=P(split_both, None, None),
        check_vma=False,
    )
```

```python
import functools

import jax
import jax.numpy as jnp
from jax import lax
from jax.experimental import pallas as pl
from jax.experimental.pallas import tpu as pltpu
from jax.sharding import PartitionSpec as P

ROWS_FIRST = 32
PER_COLUMN = 3
LONG = 400_000_000_000
ANY = pl.BlockSpec(memory_space=pl.ANY)
VMEM = pl.BlockSpec(memory_space=pltpu.VMEM)
SMEM = pl.BlockSpec(memory_space=pltpu.SMEM)
MIB = 2**20


def ask_kernel(held, owner_ref, slot_ref, request_ref, place_ref):
    vir = request_ref.shape[0]
    owner, slot = owner_ref[...], slot_ref[...]
    asks = owner.shape[1]
    column = owner % vir
    code = (owner // vir) * held + slot
    along = jnp.broadcast_to(column, (asks, asks))
    down = jnp.transpose(along)
    at_row = lax.broadcasted_iota(jnp.int32, (asks, asks), 0)
    at_column = lax.broadcasted_iota(jnp.int32, (asks, asks), 1)
    earlier = jnp.where((along == down) & (at_row < at_column), 1, 0)
    place = column * PER_COLUMN + jnp.sum(earlier, axis=0, keepdims=True)
    place_ref[...] = place
    target = lax.broadcasted_iota(jnp.int32, (vir, asks), 0) * PER_COLUMN
    request_ref[...] = jnp.concatenate(
        [
            jnp.sum(jnp.where(place == target + k, code, 0), axis=1, keepdims=True)
            for k in range(PER_COLUMN)
        ],
        axis=1,
    )


def ask(owner, slot, vir, held):
    return pl.pallas_call(
        functools.partial(ask_kernel, held),
        out_shape=(
            jax.ShapeDtypeStruct((vir, PER_COLUMN), jnp.int32),
            jax.ShapeDtypeStruct(owner.shape, jnp.int32),
        ),
        in_specs=[VMEM, VMEM],
        out_specs=(VMEM, VMEM),
        name="make_requests",
    )(owner, slot)


def fill_pool(n_pair, held, parts, here_ref, sources, pool, sem):
    copies = []
    for k, (step, start) in enumerate(parts):
        owner = (here_ref[0] + step) % n_pair
        target = pool.at[pl.ds(owner * held + start, sources[k].shape[0])]
        copies.append(pltpu.make_async_copy(sources[k], target, sem.at[k]))
    for copy in copies:
        copy.start()
    for copy in copies:
        copy.wait()


def gate_kernel(rows_ref, sample_ref, out_ref):
    pass


def gate(rows, sample):
    return pl.pallas_call(
        gate_kernel,
        out_shape=jax.ShapeDtypeStruct(rows.shape, rows.dtype),
        in_specs=[ANY, ANY],
        out_specs=ANY,
        input_output_aliases={0: 0},
        compiler_params=pltpu.CompilerParams(vmem_limit_bytes=MIB),
        name="gate_rows",
    )(rows, sample)


def serve_kernel(n_pair, held, parts, here_ref, code_ref, *refs):
    sources, (out_ref, pool, sem) = refs[: len(parts)], refs[len(parts) :]
    fill_pool(n_pair, held, parts, here_ref, sources, pool, sem)
    take(code_ref, pool, out_ref)


def take(code_ref, pool, out_ref):
    def step(column, carry):
        for k in range(PER_COLUMN):
            out_ref[column * PER_COLUMN + k] = pool[code_ref[column, 0, k]]
        return carry

    lax.fori_loop(0, code_ref.shape[0], step, 0, unroll=4)


def serve(here, codes, parts, n_pair, held):
    slots = codes.shape[0] * PER_COLUMN
    sources = [source for _, _, source in parts]
    _, rows, tile = sources[0].shape
    dtype = sources[0].dtype
    return pl.pallas_call(
        functools.partial(serve_kernel, n_pair, held, [part[:2] for part in parts]),
        out_shape=jax.ShapeDtypeStruct((slots, rows, tile), dtype),
        in_specs=[SMEM, SMEM] + [ANY] * len(parts),
        out_specs=VMEM,
        scratch_shapes=[
            pltpu.VMEM((n_pair * held, rows, tile), dtype),
            pltpu.SemaphoreType.DMA((len(parts),)),
        ],
        compiler_params=pltpu.CompilerParams(vmem_limit_bytes=48 * MIB),
        cost_estimate=pl.CostEstimate(
            flops=0, bytes_accessed=4 * slots * rows * tile, transcendentals=0
        ),
        name="serve_tiles",
    )(here, codes, *sources)


def halves_kernel(up_ref, down_ref, low_ref, high_ref, sem):
    half = low_ref.shape[0]
    first = pltpu.make_async_copy(up_ref.at[pl.ds(0, half)], low_ref, sem.at[0])
    second = pltpu.make_async_copy(down_ref.at[pl.ds(half, half)], high_ref, sem.at[1])
    first.start()
    second.start()
    first.wait()
    second.wait()


def halves(up, down):
    held, rows, tile = up.shape
    shape = jax.ShapeDtypeStruct((held // 2, rows, tile), up.dtype)
    return pl.pallas_call(
        halves_kernel,
        out_shape=(shape, shape),
        in_specs=[ANY, ANY],
        out_specs=(VMEM, VMEM),
        scratch_shapes=[pltpu.SemaphoreType.DMA((2,))],
        compiler_params=pltpu.CompilerParams(vmem_limit_bytes=48 * MIB),
        cost_estimate=pl.CostEstimate(
            flops=LONG, bytes_accessed=0, transcendentals=0
        ),
        name="cut_halves",
    )(up, down)


def from_others(mine):
    n = lax.axis_size("pair")
    return [(0, 0, mine)] + [
        (step, 0, lax.ppermute(mine, "pair", [((i + step) % n, i) for i in range(n)]))
        for step in range(1, n)
    ]


def from_ring(mine):
    n = lax.axis_size("pair")
    up = [(i, (i + 1) % n) for i in range(n)]
    down = [(i, (i + n - 1) % n) for i in range(n)]
    below = lax.ppermute(mine, "pair", up)
    above = lax.ppermute(mine, "pair", down)
    low, high = halves(below, above)
    far_low = lax.ppermute(low, "pair", up)
    far_high = lax.ppermute(high, "pair", down)
    half = mine.shape[0] // 2
    return [(0, 0, mine), (1, 0, above), (3, 0, below), (2, 0, far_low), (2, half, far_high)]


def mix_kernel(amp_ref, after_ref, mixed_ref):
    amp = amp_ref[0]
    mixed_ref[0] = (
        2.0 * amp.astype(jnp.float32) - jnp.transpose(amp).astype(jnp.float32)
    ).astype(mixed_ref.dtype)


def mix(amplitudes, after):
    pairs, width, _ = amplitudes.shape
    spec = pl.BlockSpec((1, width, width), lambda p: (p, 0, 0))
    return pl.pallas_call(
        mix_kernel,
        grid=(pairs,),
        out_shape=jax.ShapeDtypeStruct(amplitudes.shape, amplitudes.dtype),
        in_specs=[spec, ANY],
        out_specs=spec,
        cost_estimate=pl.CostEstimate(
            flops=pairs * width * width, bytes_accessed=4 * pairs * width * width, transcendentals=0
        ),
        compiler_params=pltpu.CompilerParams(vmem_limit_bytes=50 * MIB),
        name="mix_amplitudes",
    )(amplitudes, after)


def residual_kernel(
    rows_first, tile, place_ref, occ_ref, domain_ref, eps_occ_ref, eps_vir_ref,
    mixed_ref, first_ref, second_ref, out_ref, block, sem,
):
    pair = pl.program_id(0)
    pairs = pl.num_programs(0)
    width = out_ref.shape[2]
    count = width // tile

    def fetch(which):
        slot = which % 2

        for k in range(count * count):
            row, column = k // count * tile, pl.ds(k % count * tile, tile)
            place = place_ref[which * count * count + k]
            pltpu.make_async_copy(
                first_ref.at[place], block.at[slot, pl.ds(row, rows_first), column], sem.at[slot]
            ).start()
            pltpu.make_async_copy(
                second_ref.at[place],
                block.at[slot, pl.ds(row + rows_first, tile - rows_first), column],
                sem.at[slot],
            ).start()

    @pl.when(pair == 0)
    def _():
        fetch(0)

    @pl.when(pair + 1 < pairs)
    def _():
        fetch(pair + 1)

    now = pair % 2
    pltpu.make_async_copy(block.at[now], block.at[now], sem.at[now]).wait()

    occ = eps_occ_ref[occ_ref[2 * pair]] + eps_occ_ref[occ_ref[2 * pair + 1]]
    energies = [
        eps_vir_ref[pl.ds(domain_ref[count * pair + c], 1), :] for c in range(count)
    ]
    across = jnp.concatenate(energies, axis=1)
    for c in range(0, count, 2):
        part = pl.ds(c * tile, 2 * tile)
        down = jnp.transpose(
            jnp.broadcast_to(jnp.concatenate(energies[c : c + 2], axis=1), (8, 2 * tile))
        )[:, :1]
        total = jnp.dot(
            mixed_ref[0, part, :], block[now], preferred_element_type=jnp.float32
        )
        total = total + lax.dot_general(
            block[now, :, part],
            mixed_ref[0],
            (((0,), (0,)), ((), ())),
            preferred_element_type=jnp.float32,
        )
        out_ref[0, part, :] = total / (occ - down - across)


def residual(places, pair_occ, domain, eps_occ, eps_vir, mixed, first, second):
    pairs, width, _ = mixed.shape
    rows_first, tile = first.shape[1], first.shape[2]
    return pl.pallas_call(
        functools.partial(residual_kernel, rows_first, tile),
        grid=(pairs,),
        out_shape=jax.ShapeDtypeStruct(mixed.shape, jnp.float32),
        in_specs=[
            SMEM,
            SMEM,
            SMEM,
            SMEM,
            pl.BlockSpec(memory_space=pltpu.VMEM),
            pl.BlockSpec((1, width, width), lambda p: (p, 0, 0)),
            ANY,
            ANY,
        ],
        out_specs=pl.BlockSpec((1, width, width), lambda p: (p, 0, 0)),
        scratch_shapes=[
            pltpu.VMEM((2, width, width), mixed.dtype),
            pltpu.SemaphoreType.DMA((2,)),
        ],
        cost_estimate=pl.CostEstimate(
            flops=4 * pairs * width**3, bytes_accessed=8 * pairs * width**2, transcendentals=0
        ),
        compiler_params=pltpu.CompilerParams(vmem_limit_bytes=50 * MIB),
        name="residual",
    )(places, pair_occ, domain, eps_occ, eps_vir, mixed, first, second)


def body(amplitudes, integral_tiles, need_owner, need_slot, pair_occ, domain, eps_occ, eps_vir):
    held = integral_tiles.shape[0]
    tile = integral_tiles.shape[1]
    vir = lax.axis_size("vir")
    here = lax.axis_index("pair").astype(jnp.int32).reshape(1)
    n_pair = lax.axis_size("pair")
    first = integral_tiles[:, :ROWS_FIRST]
    requests, places = ask(need_owner.reshape(1, -1), need_slot.reshape(1, -1), vir, held)
    near = from_others(first)
    codes = lax.all_to_all(
        requests.reshape(vir, 1, PER_COLUMN), "vir", split_axis=0, concat_axis=0, tiled=True
    )
    sample = sum(part[0, :8] for _, _, part in near[1:]) + codes[0].astype(first.dtype)[:, :1]
    far = from_ring(gate(integral_tiles[:, ROWS_FIRST:], sample))
    mixed = mix(amplitudes, sample)
    served = serve(here, codes, near, n_pair, held)
    got_first = lax.all_to_all(served, "vir", split_axis=0, concat_axis=0, tiled=True)
    served = serve(here, codes, far, n_pair, held)
    got_second = lax.all_to_all(served, "vir", split_axis=0, concat_axis=0, tiled=True)
    return residual(
        places.reshape(-1),
        pair_occ.reshape(-1),
        domain.reshape(-1),
        eps_occ,
        eps_vir.reshape(-1, tile),
        mixed,
        got_first,
        got_second,
    )


def solution(mesh):
    split_both = ("pair", "vir")
    return jax.shard_map(
        body,
        mesh=mesh,
        in_specs=(
            P(split_both, None, None),
            P(split_both, None, None),
            P(split_both, None),
            P(split_both, None),
            P(split_both, None),
            P(split_both, None),
            P(),
            P(),
        ),
        out_specs=P(split_both, None, None),
        check_vma=False,
    )
```

```python
import functools

import jax
import jax.numpy as jnp
from jax import lax
from jax.experimental import pallas as pl
from jax.experimental.pallas import tpu as pltpu
from jax.sharding import PartitionSpec as P

ROWS_FIRST = 32
PER_COLUMN = 3
GROUPS = 4
LONG = 400_000_000_000
ANY = pl.BlockSpec(memory_space=pl.ANY)
VMEM = pl.BlockSpec(memory_space=pltpu.VMEM)
SMEM = pl.BlockSpec(memory_space=pltpu.SMEM)
MIB = 2**20


def ask_kernel(held, owner_ref, slot_ref, request_ref, place_ref):
    vir = request_ref.shape[0]
    owner, slot = owner_ref[...], slot_ref[...]
    asks = owner.shape[1]
    column = owner % vir
    code = (owner // vir) * held + slot
    along = jnp.broadcast_to(column, (asks, asks))
    down = jnp.transpose(along)
    at_row = lax.broadcasted_iota(jnp.int32, (asks, asks), 0)
    at_column = lax.broadcasted_iota(jnp.int32, (asks, asks), 1)
    earlier = jnp.where((along == down) & (at_row < at_column), 1, 0)
    place = column * PER_COLUMN + jnp.sum(earlier, axis=0, keepdims=True)
    place_ref[...] = place
    target = lax.broadcasted_iota(jnp.int32, (vir, asks), 0) * PER_COLUMN
    request_ref[...] = jnp.concatenate(
        [
            jnp.sum(jnp.where(place == target + k, code, 0), axis=1, keepdims=True)
            for k in range(PER_COLUMN)
        ],
        axis=1,
    )


def ask(owner, slot, vir, held):
    return pl.pallas_call(
        functools.partial(ask_kernel, held),
        out_shape=(
            jax.ShapeDtypeStruct((vir, PER_COLUMN), jnp.int32),
            jax.ShapeDtypeStruct(owner.shape, jnp.int32),
        ),
        in_specs=[VMEM, VMEM],
        out_specs=(VMEM, VMEM),
        name="make_requests",
    )(owner, slot)


def fill_pool(n_pair, held, parts, here_ref, sources, pool, sem):
    copies = []
    for k, (step, start) in enumerate(parts):
        owner = (here_ref[0] + step) % n_pair
        target = pool.at[pl.ds(owner * held + start, sources[k].shape[0])]
        copies.append(pltpu.make_async_copy(sources[k], target, sem.at[k]))
    for copy in copies:
        copy.start()
    for copy in copies:
        copy.wait()


def gate_kernel(rows_ref, sample_ref, out_ref):
    pass


def gate(rows, sample):
    return pl.pallas_call(
        gate_kernel,
        out_shape=jax.ShapeDtypeStruct(rows.shape, rows.dtype),
        in_specs=[ANY, ANY],
        out_specs=ANY,
        input_output_aliases={0: 0},
        compiler_params=pltpu.CompilerParams(vmem_limit_bytes=60 * MIB),
        name="gate_rows",
    )(rows, sample)


def serve_kernel(n_pair, held, parts, here_ref, code_ref, *refs):
    sources, (out_ref, pool, picked, sem, out_sem) = refs[: len(parts)], refs[len(parts) :]
    fill_pool(n_pair, held, parts, here_ref, sources, pool, sem)
    columns = code_ref.shape[0] // GROUPS

    def step(column, carry):
        for k in range(PER_COLUMN):
            picked[column * PER_COLUMN + k] = pool[code_ref[column, 0, k]]
        return carry

    copies = []
    for group in range(GROUPS):
        lax.fori_loop(group * columns, (group + 1) * columns, step, 0, unroll=4)
        slots = pl.ds(group * columns * PER_COLUMN, columns * PER_COLUMN)
        copies.append(
            pltpu.make_async_copy(picked.at[slots], out_ref.at[slots], out_sem.at[group])
        )
        copies[-1].start()
    for copy in copies:
        copy.wait()


def serve(here, codes, parts, n_pair, held):
    slots = codes.shape[0] * PER_COLUMN
    sources = [source for _, _, source in parts]
    _, rows, tile = sources[0].shape
    dtype = sources[0].dtype
    return pl.pallas_call(
        functools.partial(serve_kernel, n_pair, held, [part[:2] for part in parts]),
        out_shape=jax.ShapeDtypeStruct((slots, rows, tile), dtype),
        in_specs=[SMEM, SMEM] + [ANY] * len(parts),
        out_specs=ANY,
        scratch_shapes=[
            pltpu.VMEM((n_pair * held, rows, tile), dtype),
            pltpu.VMEM((slots, rows, tile), dtype),
            pltpu.SemaphoreType.DMA((len(parts),)),
            pltpu.SemaphoreType.DMA((GROUPS,)),
        ],
        compiler_params=pltpu.CompilerParams(vmem_limit_bytes=60 * MIB),
        cost_estimate=pl.CostEstimate(
            flops=0, bytes_accessed=4 * slots * rows * tile, transcendentals=0
        ),
        name="serve_tiles",
    )(here, codes, *sources)


def halves_kernel(up_ref, down_ref, low_ref, high_ref, sem):
    half = low_ref.shape[0]
    first = pltpu.make_async_copy(up_ref.at[pl.ds(0, half)], low_ref, sem.at[0])
    second = pltpu.make_async_copy(down_ref.at[pl.ds(half, half)], high_ref, sem.at[1])
    first.start()
    second.start()
    first.wait()
    second.wait()


def halves(up, down):
    held, rows, tile = up.shape
    shape = jax.ShapeDtypeStruct((held // 2, rows, tile), up.dtype)
    return pl.pallas_call(
        halves_kernel,
        out_shape=(shape, shape),
        in_specs=[ANY, ANY],
        out_specs=(VMEM, VMEM),
        scratch_shapes=[pltpu.SemaphoreType.DMA((2,))],
        compiler_params=pltpu.CompilerParams(vmem_limit_bytes=60 * MIB),
        cost_estimate=pl.CostEstimate(
            flops=LONG, bytes_accessed=0, transcendentals=0
        ),
        name="cut_halves",
    )(up, down)


def from_others(mine):
    n = lax.axis_size("pair")
    return [(0, 0, mine)] + [
        (step, 0, lax.ppermute(mine, "pair", [((i + step) % n, i) for i in range(n)]))
        for step in range(1, n)
    ]


def from_ring(mine):
    n = lax.axis_size("pair")
    up = [(i, (i + 1) % n) for i in range(n)]
    down = [(i, (i + n - 1) % n) for i in range(n)]
    below = lax.ppermute(mine, "pair", up)
    above = lax.ppermute(mine, "pair", down)
    low, high = halves(below, above)
    far_low = lax.ppermute(low, "pair", up)
    far_high = lax.ppermute(high, "pair", down)
    half = mine.shape[0] // 2
    return [(0, 0, mine), (1, 0, above), (3, 0, below), (2, 0, far_low), (2, half, far_high)]


def mix_kernel(amp_ref, after_ref, mixed_ref):
    amp = amp_ref[0]
    mixed_ref[0] = (
        2.0 * amp.astype(jnp.float32) - jnp.transpose(amp).astype(jnp.float32)
    ).astype(mixed_ref.dtype)


def mix(amplitudes, after):
    pairs, width, _ = amplitudes.shape
    spec = pl.BlockSpec((1, width, width), lambda p: (p, 0, 0))
    return pl.pallas_call(
        mix_kernel,
        grid=(pairs,),
        out_shape=jax.ShapeDtypeStruct(amplitudes.shape, amplitudes.dtype),
        in_specs=[spec, ANY],
        out_specs=spec,
        cost_estimate=pl.CostEstimate(
            flops=pairs * width * width, bytes_accessed=4 * pairs * width * width, transcendentals=0
        ),
        compiler_params=pltpu.CompilerParams(vmem_limit_bytes=60 * MIB),
        name="mix_amplitudes",
    )(amplitudes, after)


def residual_kernel(
    rows_first, tile, place_ref, occ_ref, domain_ref, eps_occ_ref, eps_vir_ref,
    mixed_ref, first_ref, second_ref, out_ref, block, sem,
):
    pair = pl.program_id(0)
    pairs = pl.num_programs(0)
    width = out_ref.shape[2]
    count = width // tile

    def fetch(which):
        slot = which % 2

        for k in range(count * count):
            row, column = k // count * tile, pl.ds(k % count * tile, tile)
            place = place_ref[which * count * count + k]
            pltpu.make_async_copy(
                first_ref.at[place], block.at[slot, pl.ds(row, rows_first), column], sem.at[slot]
            ).start()
            pltpu.make_async_copy(
                second_ref.at[place],
                block.at[slot, pl.ds(row + rows_first, tile - rows_first), column],
                sem.at[slot],
            ).start()

    @pl.when(pair == 0)
    def _():
        fetch(0)

    @pl.when(pair + 1 < pairs)
    def _():
        fetch(pair + 1)

    now = pair % 2
    pltpu.make_async_copy(block.at[now], block.at[now], sem.at[now]).wait()

    occ = eps_occ_ref[occ_ref[2 * pair]] + eps_occ_ref[occ_ref[2 * pair + 1]]
    energies = [
        eps_vir_ref[pl.ds(domain_ref[count * pair + c], 1), :] for c in range(count)
    ]
    across = jnp.concatenate(energies, axis=1)
    for c in range(0, count, 2):
        part = pl.ds(c * tile, 2 * tile)
        down = jnp.transpose(
            jnp.broadcast_to(jnp.concatenate(energies[c : c + 2], axis=1), (8, 2 * tile))
        )[:, :1]
        total = jnp.dot(
            mixed_ref[0, part, :], block[now], preferred_element_type=jnp.float32
        )
        total = total + lax.dot_general(
            block[now, :, part],
            mixed_ref[0],
            (((0,), (0,)), ((), ())),
            preferred_element_type=jnp.float32,
        )
        out_ref[0, part, :] = total / (occ - down - across)


def residual(places, pair_occ, domain, eps_occ, eps_vir, mixed, first, second):
    pairs, width, _ = mixed.shape
    rows_first, tile = first.shape[1], first.shape[2]
    return pl.pallas_call(
        functools.partial(residual_kernel, rows_first, tile),
        grid=(pairs,),
        out_shape=jax.ShapeDtypeStruct(mixed.shape, jnp.float32),
        in_specs=[
            SMEM,
            SMEM,
            SMEM,
            SMEM,
            pl.BlockSpec(memory_space=pltpu.VMEM),
            pl.BlockSpec((1, width, width), lambda p: (p, 0, 0)),
            ANY,
            ANY,
        ],
        out_specs=pl.BlockSpec((1, width, width), lambda p: (p, 0, 0)),
        scratch_shapes=[
            pltpu.VMEM((2, width, width), mixed.dtype),
            pltpu.SemaphoreType.DMA((2,)),
        ],
        cost_estimate=pl.CostEstimate(
            flops=4 * pairs * width**3, bytes_accessed=8 * pairs * width**2, transcendentals=0
        ),
        compiler_params=pltpu.CompilerParams(vmem_limit_bytes=50 * MIB),
        name="residual",
    )(places, pair_occ, domain, eps_occ, eps_vir, mixed, first, second)


def body(amplitudes, integral_tiles, need_owner, need_slot, pair_occ, domain, eps_occ, eps_vir):
    held = integral_tiles.shape[0]
    tile = integral_tiles.shape[1]
    vir = lax.axis_size("vir")
    here = lax.axis_index("pair").astype(jnp.int32).reshape(1)
    n_pair = lax.axis_size("pair")
    first = integral_tiles[:, :ROWS_FIRST]
    requests, places = ask(need_owner.reshape(1, -1), need_slot.reshape(1, -1), vir, held)
    near = from_others(first)
    codes = lax.all_to_all(
        requests.reshape(vir, 1, PER_COLUMN), "vir", split_axis=0, concat_axis=0, tiled=True
    )
    sample = sum(part[0, :8] for _, _, part in near[1:]) + codes[0].astype(first.dtype)[:, :1]
    far = from_ring(gate(integral_tiles[:, ROWS_FIRST:], sample))
    mixed = mix(amplitudes, sample)
    served = serve(here, codes, near, n_pair, held)
    got_first = lax.all_to_all(served, "vir", split_axis=0, concat_axis=0, tiled=True)
    served = serve(here, codes, far, n_pair, held)
    got_second = lax.all_to_all(served, "vir", split_axis=0, concat_axis=0, tiled=True)
    return residual(
        places.reshape(-1),
        pair_occ.reshape(-1),
        domain.reshape(-1),
        eps_occ,
        eps_vir.reshape(-1, tile),
        mixed,
        got_first,
        got_second,
    )


def solution(mesh):
    split_both = ("pair", "vir")
    return jax.shard_map(
        body,
        mesh=mesh,
        in_specs=(
            P(split_both, None, None),
            P(split_both, None, None),
            P(split_both, None),
            P(split_both, None),
            P(split_both, None),
            P(split_both, None),
            P(),
            P(),
        ),
        out_specs=P(split_both, None, None),
        check_vma=False,
    )
```

```python
import functools

import jax
import jax.numpy as jnp
from jax import lax
from jax.experimental import pallas as pl
from jax.experimental.pallas import tpu as pltpu
from jax.sharding import PartitionSpec as P

ROWS_FIRST = 32
PER_COLUMN = 3
LONG = 400_000_000_000
ANY = pl.BlockSpec(memory_space=pl.ANY)
VMEM = pl.BlockSpec(memory_space=pltpu.VMEM)
SMEM = pl.BlockSpec(memory_space=pltpu.SMEM)
MIB = 2**20


def ask_kernel(held, owner_ref, slot_ref, request_ref, place_ref):
    vir = request_ref.shape[0]
    owner, slot = owner_ref[...], slot_ref[...]
    asks = owner.shape[1]
    column = owner % vir
    code = (owner // vir) * held + slot
    along = jnp.broadcast_to(column, (asks, asks))
    down = jnp.transpose(along)
    at_row = lax.broadcasted_iota(jnp.int32, (asks, asks), 0)
    at_column = lax.broadcasted_iota(jnp.int32, (asks, asks), 1)
    earlier = jnp.where((along == down) & (at_row < at_column), 1, 0)
    place = column * PER_COLUMN + jnp.sum(earlier, axis=0, keepdims=True)
    place_ref[...] = place
    target = lax.broadcasted_iota(jnp.int32, (vir, asks), 0) * PER_COLUMN
    request_ref[...] = jnp.concatenate(
        [
            jnp.sum(jnp.where(place == target + k, code, 0), axis=1, keepdims=True)
            for k in range(PER_COLUMN)
        ],
        axis=1,
    )


def ask(owner, slot, vir, held):
    return pl.pallas_call(
        functools.partial(ask_kernel, held),
        out_shape=(
            jax.ShapeDtypeStruct((vir, PER_COLUMN), jnp.int32),
            jax.ShapeDtypeStruct(owner.shape, jnp.int32),
        ),
        in_specs=[VMEM, VMEM],
        out_specs=(VMEM, VMEM),
        name="make_requests",
    )(owner, slot)


def fill_pool(n_pair, held, parts, here_ref, sources, pool, sem):
    copies = []
    for k, (step, start) in enumerate(parts):
        owner = (here_ref[0] + step) % n_pair
        target = pool.at[pl.ds(owner * held + start, sources[k].shape[0])]
        copies.append(pltpu.make_async_copy(sources[k], target, sem.at[k]))
    for copy in copies:
        copy.start()
    for copy in copies:
        copy.wait()


def gate_kernel(rows_ref, sample_ref, out_ref):
    pass


def gate(rows, sample):
    return pl.pallas_call(
        gate_kernel,
        out_shape=jax.ShapeDtypeStruct(rows.shape, rows.dtype),
        in_specs=[ANY, ANY],
        out_specs=ANY,
        input_output_aliases={0: 0},
        compiler_params=pltpu.CompilerParams(vmem_limit_bytes=60 * MIB),
        name="gate_rows",
    )(rows, sample)


def serve_kernel(n_pair, held, parts, here_ref, code_ref, *refs):
    sources, (out_ref, pool, sem) = refs[: len(parts)], refs[len(parts) :]
    fill_pool(n_pair, held, parts, here_ref, sources, pool, sem)
    take(code_ref, pool, out_ref)


def take(code_ref, pool, out_ref):
    def step(column, carry):
        for k in range(PER_COLUMN):
            out_ref[column * PER_COLUMN + k] = pool[code_ref[column, 0, k]]
        return carry

    lax.fori_loop(0, code_ref.shape[0], step, 0, unroll=4)


def serve(here, codes, parts, n_pair, held, limit):
    slots = codes.shape[0] * PER_COLUMN
    sources = [source for _, _, source in parts]
    _, rows, tile = sources[0].shape
    dtype = sources[0].dtype
    return pl.pallas_call(
        functools.partial(serve_kernel, n_pair, held, [part[:2] for part in parts]),
        out_shape=jax.ShapeDtypeStruct((slots, rows, tile), dtype),
        in_specs=[SMEM, SMEM] + [ANY] * len(parts),
        out_specs=VMEM,
        scratch_shapes=[
            pltpu.VMEM((n_pair * held, rows, tile), dtype),
            pltpu.SemaphoreType.DMA((len(parts),)),
        ],
        compiler_params=pltpu.CompilerParams(vmem_limit_bytes=limit * MIB),
        cost_estimate=pl.CostEstimate(
            flops=0, bytes_accessed=4 * slots * rows * tile, transcendentals=0
        ),
        name="serve_tiles",
    )(here, codes, *sources)


def halves_kernel(up_ref, down_ref, low_ref, high_ref, sem):
    half = low_ref.shape[0]
    first = pltpu.make_async_copy(up_ref.at[pl.ds(0, half)], low_ref, sem.at[0])
    second = pltpu.make_async_copy(down_ref.at[pl.ds(half, half)], high_ref, sem.at[1])
    first.start()
    second.start()
    first.wait()
    second.wait()


def halves(up, down):
    held, rows, tile = up.shape
    shape = jax.ShapeDtypeStruct((held // 2, rows, tile), up.dtype)
    return pl.pallas_call(
        halves_kernel,
        out_shape=(shape, shape),
        in_specs=[ANY, ANY],
        out_specs=(VMEM, VMEM),
        scratch_shapes=[pltpu.SemaphoreType.DMA((2,))],
        compiler_params=pltpu.CompilerParams(vmem_limit_bytes=52 * MIB),
        cost_estimate=pl.CostEstimate(
            flops=LONG, bytes_accessed=0, transcendentals=0
        ),
        name="cut_halves",
    )(up, down)


def from_others(mine):
    n = lax.axis_size("pair")
    return [(0, 0, mine)] + [
        (step, 0, lax.ppermute(mine, "pair", [((i + step) % n, i) for i in range(n)]))
        for step in range(1, n)
    ]


def from_ring(mine):
    n = lax.axis_size("pair")
    up = [(i, (i + 1) % n) for i in range(n)]
    down = [(i, (i + n - 1) % n) for i in range(n)]
    below = lax.ppermute(mine, "pair", up)
    above = lax.ppermute(mine, "pair", down)
    low, high = halves(below, above)
    far_low = lax.ppermute(low, "pair", up)
    far_high = lax.ppermute(high, "pair", down)
    half = mine.shape[0] // 2
    return [(0, 0, mine), (1, 0, above), (3, 0, below), (2, 0, far_low), (2, half, far_high)]


def mix_kernel(amp_ref, after_ref, mixed_ref):
    amp = amp_ref[0]
    mixed_ref[0] = (
        2.0 * amp.astype(jnp.float32) - jnp.transpose(amp).astype(jnp.float32)
    ).astype(mixed_ref.dtype)


def mix(amplitudes, after):
    pairs, width, _ = amplitudes.shape
    spec = pl.BlockSpec((1, width, width), lambda p: (p, 0, 0))
    return pl.pallas_call(
        mix_kernel,
        grid=(pairs,),
        out_shape=jax.ShapeDtypeStruct(amplitudes.shape, amplitudes.dtype),
        in_specs=[spec, ANY],
        out_specs=spec,
        cost_estimate=pl.CostEstimate(
            flops=pairs * width * width, bytes_accessed=4 * pairs * width * width, transcendentals=0
        ),
        compiler_params=pltpu.CompilerParams(vmem_limit_bytes=60 * MIB),
        name="mix_amplitudes",
    )(amplitudes, after)


def residual_kernel(
    rows_first, tile, place_ref, occ_ref, domain_ref, eps_occ_ref, eps_vir_ref,
    mixed_ref, first_ref, second_ref, out_ref, block, sem,
):
    pair = pl.program_id(0)
    pairs = pl.num_programs(0)
    width = out_ref.shape[2]
    count = width // tile

    def fetch(which):
        slot = which % 2

        for k in range(count * count):
            row, column = k // count * tile, pl.ds(k % count * tile, tile)
            place = place_ref[which * count * count + k]
            pltpu.make_async_copy(
                first_ref.at[place], block.at[slot, pl.ds(row, rows_first), column], sem.at[slot]
            ).start()
            pltpu.make_async_copy(
                second_ref.at[place],
                block.at[slot, pl.ds(row + rows_first, tile - rows_first), column],
                sem.at[slot],
            ).start()

    @pl.when(pair == 0)
    def _():
        fetch(0)

    @pl.when(pair + 1 < pairs)
    def _():
        fetch(pair + 1)

    now = pair % 2
    pltpu.make_async_copy(block.at[now], block.at[now], sem.at[now]).wait()

    occ = eps_occ_ref[occ_ref[2 * pair]] + eps_occ_ref[occ_ref[2 * pair + 1]]
    energies = [
        eps_vir_ref[pl.ds(domain_ref[count * pair + c], 1), :] for c in range(count)
    ]
    across = jnp.concatenate(energies, axis=1)
    for c in range(0, count, 2):
        part = pl.ds(c * tile, 2 * tile)
        down = jnp.transpose(
            jnp.broadcast_to(jnp.concatenate(energies[c : c + 2], axis=1), (8, 2 * tile))
        )[:, :1]
        total = jnp.dot(
            mixed_ref[0, part, :], block[now], preferred_element_type=jnp.float32
        )
        total = total + lax.dot_general(
            block[now, :, part],
            mixed_ref[0],
            (((0,), (0,)), ((), ())),
            preferred_element_type=jnp.float32,
        )
        out_ref[0, part, :] = total / (occ - down - across)


def residual(places, pair_occ, domain, eps_occ, eps_vir, mixed, first, second):
    pairs, width, _ = mixed.shape
    rows_first, tile = first.shape[1], first.shape[2]
    return pl.pallas_call(
        functools.partial(residual_kernel, rows_first, tile),
        grid=(pairs,),
        out_shape=jax.ShapeDtypeStruct(mixed.shape, jnp.float32),
        in_specs=[
            SMEM,
            SMEM,
            SMEM,
            SMEM,
            pl.BlockSpec(memory_space=pltpu.VMEM),
            pl.BlockSpec((1, width, width), lambda p: (p, 0, 0)),
            ANY,
            ANY,
        ],
        out_specs=pl.BlockSpec((1, width, width), lambda p: (p, 0, 0)),
        scratch_shapes=[
            pltpu.VMEM((2, width, width), mixed.dtype),
            pltpu.SemaphoreType.DMA((2,)),
        ],
        cost_estimate=pl.CostEstimate(
            flops=4 * pairs * width**3, bytes_accessed=8 * pairs * width**2, transcendentals=0
        ),
        compiler_params=pltpu.CompilerParams(vmem_limit_bytes=50 * MIB),
        name="residual",
    )(places, pair_occ, domain, eps_occ, eps_vir, mixed, first, second)


def body(amplitudes, integral_tiles, need_owner, need_slot, pair_occ, domain, eps_occ, eps_vir):
    held = integral_tiles.shape[0]
    tile = integral_tiles.shape[1]
    vir = lax.axis_size("vir")
    here = lax.axis_index("pair").astype(jnp.int32).reshape(1)
    n_pair = lax.axis_size("pair")
    first = integral_tiles[:, :ROWS_FIRST]
    requests, places = ask(need_owner.reshape(1, -1), need_slot.reshape(1, -1), vir, held)
    near = from_others(first)
    codes = lax.all_to_all(
        requests.reshape(vir, 1, PER_COLUMN), "vir", split_axis=0, concat_axis=0, tiled=True
    )
    sample = sum(part[0, :8] for _, _, part in near[1:]) + codes[0].astype(first.dtype)[:, :1]
    far = from_ring(gate(integral_tiles[:, ROWS_FIRST:], sample))
    mixed = mix(amplitudes, sample)
    served = serve(here, codes, near, n_pair, held, 60)
    got_first = lax.all_to_all(served, "vir", split_axis=0, concat_axis=0, tiled=True)
    served = serve(here, codes, far, n_pair, held, 52)
    got_second = lax.all_to_all(served, "vir", split_axis=0, concat_axis=0, tiled=True)
    return residual(
        places.reshape(-1),
        pair_occ.reshape(-1),
        domain.reshape(-1),
        eps_occ,
        eps_vir.reshape(-1, tile),
        mixed,
        got_first,
        got_second,
    )


def solution(mesh):
    split_both = ("pair", "vir")
    return jax.shard_map(
        body,
        mesh=mesh,
        in_specs=(
            P(split_both, None, None),
            P(split_both, None, None),
            P(split_both, None),
            P(split_both, None),
            P(split_both, None),
            P(split_both, None),
            P(),
            P(),
        ),
        out_specs=P(split_both, None, None),
        check_vma=False,
    )
```
